256 devices in a mesh: dp: 4 (over y), expert: 64 (over z, x, core).
Axes of the slice: x: 4, y: 4, z: 8, core: 2. Of those that a mesh axis runs over, the one named last changes fastest.
Arguments:
- learner_hidden: bfloat16 [512, 8192], P('dp'), may hold values from -6 to 6
- learner_cot: bfloat16 [512, 7168], P('dp', 'expert'), may hold values from -0.25 to 0.25
- master: float32 [8192, 7168], P('dp', 'expert'), may hold values from -0.125 to 0.125
- moment_one: float32 [8192, 7168], P('dp', 'expert'), may hold values from -3 to 3
- moment_two: float32 [8192, 7168], P('dp', 'expert'), may hold values from 0.05 to 5
- slot_units: int32 [12288], replicated, may hold values from 0 to 8192, as said below
- gate_slots: bfloat16 [12288, 7168], P('expert'), may hold values from -0.0625 to 0.0625
- up_slots: bfloat16 [12288, 7168], P('expert'), may hold values from -0.0625 to 0.0625
- norm_gain: bfloat16 [7168], replicated, may hold values from 0.5 to 1.5
- tokens: bfloat16 [768, 7168], P(('dp', 'expert')), may hold values from -6 to 6
- routes: int32 [768, 2], P(('dp', 'expert')), may hold values from 0 to 3, all different within a row
- gate_weights: bfloat16 [768, 2], P(('dp', 'expert')), may hold values from 0.19921875 to 1
Outputs:
- master_new: float32 [8192, 7168], P('dp', 'expert')
- moment_new: float32 [8192, 7168], P('dp', 'expert')
- second_new: float32 [8192, 7168], P('dp', 'expert')
- decoded: bfloat16 [768, 7168], P(('dp', 'expert'))
The draws below stay inside these ranges and needn't reach their ends.
Inputs may be any that keep to these rules, and one draw needn't show every extreme that they name: `slot_units`: each of the 8192 units stands in exactly one slot. The 192 slots of each owner hold a run of consecutive units in rising order followed by empty slots marked 8192; every owner holds between 64 and 192 units, and some owner holds 192.
All inputs are finite; a program needn't handle non-finite values.
Results may differ from the reference program's by a relative error of at most 0.012.
Values may be sent and summed in bfloat16 or wider, within the bound.
No kernel may reach another device: no remote copies, remote signals or barrier semaphores. Data moves between devices by JAX's collectives and lax.ppermute only.
A program may use at most 128 MiB of HBM per device.

```python
import math
import jax
import jax.numpy as jnp
from jax import lax

D = 7168
FF = 2048
TOPW = 2
STEPS = 2
ADAM_STEP = 10
FLIGHT = 4
UNITS = 8192
MEAN_OWN = 128
CAP = 192
TOKL_ALL = 512
ROWS_ALL = 768
N_EXPERT = 64


def draw_slot_units(key, part):
    key = jax.random.fold_in(key, 7)
    key_counts, key_order = jax.random.split(key)
    half_owners = N_EXPERT // 2
    spread_max = MEAN_OWN // 2
    surplus = jax.random.randint(key_counts, (half_owners,), 0, spread_max + 1)
    surplus = surplus.at[0].set(spread_max)
    owner_counts = jnp.concatenate([MEAN_OWN + surplus, MEAN_OWN - surplus]).astype(jnp.int32)
    shuffled = jax.random.permutation(key_order, N_EXPERT)
    ordered = owner_counts[shuffled]
    starts_ordered = (jnp.cumsum(ordered) - ordered).astype(jnp.int32)
    offsets = jnp.zeros((N_EXPERT,), jnp.int32).at[shuffled].set(starts_ordered)
    position = jnp.arange(CAP, dtype=jnp.int32)[None, :]
    slot_table = jnp.where(position < owner_counts[:, None], offsets[:, None] + position, UNITS)
    return slot_table.reshape(-1).astype(jnp.int32)


def levels(stream_key, dims, cuts, least, top_value):
    level = 1.0
    for dim, parts in cuts:
        steps = jax.random.uniform(jax.random.fold_in(jax.random.fold_in(stream_key, 6), dim), (parts,), jnp.float32, least / len(cuts), top_value / len(cuts))
        level = level * jnp.repeat(jnp.exp(steps), dims[dim] // parts).reshape((-1,) + (1,) * (len(dims) - 1 - dim))
    return level


def distinct(stream_key, rows, count, top, lift):
    order = jax.random.permutation(jax.random.fold_in(stream_key, 1), count)
    boost = order
    for power in range(3):
        boost = boost * boost // count
    boost = boost * lift // count
    tickets = jax.random.randint(jax.random.fold_in(stream_key, 2), (rows, count), 0, 4096) + boost
    sure = jax.random.permutation(jax.random.fold_in(stream_key, 3), rows)[jnp.arange(count) % rows]
    tickets = jnp.where(jnp.arange(rows)[:, None] == sure[None, :], 1 << 14, tickets)
    merit = tickets * count + jnp.arange(count)
    return lax.top_k(merit.astype(jnp.int32), top)[1].astype(jnp.int32)


def normal_values(rng, dims, deviation, limit, shards=(), kind=jnp.bfloat16):
    result = deviation * jax.random.normal(rng, dims, jnp.float32)
    if shards:
        result = result * levels(rng, dims, shards, -0.22, 0.18)
    return jnp.clip(result, -limit, limit).astype(kind)


def setup_inputs(seed: int = 0) -> dict:
    key_of = jax.random.split(jax.random.key(seed), 13)
    learner_hidden = normal_values(key_of[0], (TOKL_ALL, UNITS), 1.0, 6.0, ((0, 4),))
    learner_cot = normal_values(key_of[1], (TOKL_ALL, D), TOKL_ALL ** -0.5, 0.25, ((0, 4), (1, 64)))
    master = normal_values(key_of[2], (UNITS, D), FF ** -0.5, 0.125, ((0, 4), (1, 64)), jnp.float32)
    moment_one = normal_values(key_of[3], (UNITS, D), 0.3, 3.0, ((0, 4), (1, 64)), jnp.float32)
    moment_two = jnp.clip(jnp.exp(math.log(5.0) - 4.6051702 * jax.random.uniform(key_of[4], (UNITS, D), jnp.float32) ** levels(key_of[4], (UNITS, D), ((0, 4), (1, 64)), -0.2, 0.2)), 0.05, 5.0)
    slot_units = draw_slot_units(jax.random.fold_in(key_of[12], 71), 0)
    gate_slots = normal_values(key_of[6], (N_EXPERT * CAP, D), D ** -0.5, 0.0625, ((0, 64),))
    up_slots = normal_values(key_of[7], (N_EXPERT * CAP, D), D ** -0.5, 0.0625, ((0, 64),))
    norm_gain = jnp.clip(1.0 + 0.1 * jax.random.normal(key_of[8], (D,), jnp.float32), 0.5, 1.5).astype(jnp.bfloat16)
    tokens = normal_values(key_of[9], (ROWS_ALL, D), 1.0, 6.0, ((0, 256),))
    routes = distinct(key_of[10], ROWS_ALL, FLIGHT, TOPW, 8192)
    gate_weights = jnp.clip(0.19921875 + 0.80078125 * jax.random.uniform(key_of[11], (ROWS_ALL, TOPW), jnp.float32) ** levels(key_of[11], (ROWS_ALL, TOPW), ((0, 256),), -0.2, 0.2), 0.19921875, 1.0).astype(jnp.bfloat16)
    return dict(learner_hidden=learner_hidden, learner_cot=learner_cot, master=master, moment_one=moment_one, moment_two=moment_two, slot_units=slot_units, gate_slots=gate_slots, up_slots=up_slots, norm_gain=norm_gain, tokens=tokens, routes=routes, gate_weights=gate_weights)


def reference(learner_hidden, learner_cot, master, moment_one, moment_two, slot_units, gate_slots, up_slots, norm_gain, tokens, routes, gate_weights):
    grad = jnp.dot(learner_hidden.T, learner_cot, preferred_element_type=jnp.float32)
    moment_new = 0.9 * moment_one + 0.1 * grad
    second_new = 0.95 * moment_two + 0.05 * grad * grad
    corr_first = 1.0 - 0.9 ** ADAM_STEP
    corr_second = 1.0 - 0.95 ** ADAM_STEP
    master_new = master - 0.005 * (moment_new / corr_first / (jnp.sqrt(second_new / corr_second) + 1e-08) + 0.1 * master)
    down = master_new.astype(jnp.bfloat16)
    slot_total = slot_units.shape[0]
    inverse = jnp.zeros((UNITS + 1,), jnp.int32).at[slot_units].set(jnp.arange(slot_total, dtype=jnp.int32))[:UNITS]
    gate_units = gate_slots[inverse]
    up_units = up_slots[inverse]
    unit_expert = jnp.arange(UNITS, dtype=jnp.int32) // FF
    expert_ids = jnp.arange(FLIGHT, dtype=jnp.int32)
    onehot = (unit_expert[:, None] == expert_ids[None, :]).astype(jnp.float32)
    picks = (routes[:, :, None] == expert_ids[None, None, :]).astype(jnp.float32)
    expert_weight = lax.optimization_barrier(jnp.sum(gate_weights.astype(jnp.float32)[:, :, None] * picks, axis=1)).astype(jnp.bfloat16)
    unit_weight = jnp.dot(expert_weight.astype(jnp.float32), onehot.T)
    current = tokens
    for step_index in range(STEPS):
        values = current.astype(jnp.float32)
        meansq = lax.optimization_barrier(jnp.mean(values * values, axis=-1, keepdims=True))
        normed = (values * jax.lax.rsqrt(meansq + 1e-06) * norm_gain.astype(jnp.float32)).astype(jnp.bfloat16)
        first = jnp.dot(normed, gate_units.T, preferred_element_type=jnp.float32)
        second = jnp.dot(normed, up_units.T, preferred_element_type=jnp.float32)
        hidden = (jax.nn.silu(first) * second * unit_weight).astype(jnp.bfloat16)
        update = jnp.dot(hidden, down, preferred_element_type=jnp.float32)
        current = (current.astype(jnp.float32) + update).astype(jnp.bfloat16)
    return (master_new, moment_new, second_new, current)
```

```python
import jax
import jax.numpy as jnp
from jax import lax
from jax.experimental import pallas as pl
from jax.experimental.pallas import tpu as pltpu
from jax.sharding import PartitionSpec as P

D = 7168
FF = 2048
STEPS = 2
ADAM_STEP = 10
UNITS = 8192
FLIGHT = 4
CAP = 192
OWNERS = 64
NZ, NX, NC, NY = 8, 4, 2, 4
CHIPS = NZ * NX
FEAT = D // OWNERS
CHIP_FEAT = D // CHIPS
CHIP_CAP = NC * CAP
BLOCK = UNITS // NY
OWN = 3
ROWS = OWN * CHIPS
TAIL = 128 - ROWS
ROW_MAIN = 176
HID_MAIN = 288
CHUNKS = D // 128
TILE = 512
EXPERT = ("z", "x", "c")
Z_ORDER = (0, 7, 1, 6, 2, 5, 3, 4, 4)
BF = jnp.bfloat16
F32 = jnp.float32


def send(value, axis, size, by):
    return lax.ppermute(value, axis, [(i, (i + by) % size) for i in range(size)])


def together(*values):
    return lax.optimization_barrier(values)


def gather_chips(shard, early=None, late=None):
    four = lax.all_to_all(
        jnp.broadcast_to(shard[None], (NX,) + shard.shape), "x", split_axis=0, concat_axis=0, tiled=True
    )
    if early is not None:
        four, early = together(four, early)
    pieces, up, down = [four], four, four
    for step in range(3):
        up, down = send(up, "z", NZ, 1), send(down, "z", NZ, -1)
        if step == 1 and late is not None:
            up, down, late = together(up, down, late)
        pieces += [up, down]
    return pieces + [send(up[:2], "z", NZ, 1), send(down[2:], "z", NZ, -1)], early, late


def each_shard(place, pieces, body):
    for i, piece in enumerate(pieces):
        plane = lax.rem(place[0] + Z_ORDER[i], NZ) * NX + (2 if i == 8 else 0)

        def step(j, carry, piece=piece, plane=plane):
            body(plane + j, piece[j])
            return carry

        lax.fori_loop(0, piece.shape[0], step, 0)


def pack(full, main):
    rest = full[main:]
    parts = [rest[:, k : k + TAIL] for k in range(0, ROWS, TAIL)]
    missing = main - 3 * rest.shape[0]
    if missing:
        parts.append(jnp.zeros((missing, TAIL), full.dtype))
    return jnp.concatenate([full[:main, :ROWS], jnp.concatenate(parts, axis=0)], axis=1)


def unpack(place, pieces, whole, size, main):
    rest = size - main

    def body(chip, shard):
        at = pl.multiple_of(chip * size, 16)
        whole[pl.ds(at, main), :] = shard
        parts = [shard[k * rest : (k + 1) * rest, ROWS:] for k in range(3)]
        whole[pl.ds(pl.multiple_of(at + main, 16), rest), :] = jnp.concatenate(
            parts + parts[:1], axis=1
        )

    each_shard(place, pieces, body)


HALF = D // 2


def weight_copies(sources, held, sems):
    return [
        [
            pltpu.make_async_copy(
                source.at[:, pl.ds(half * HALF, HALF)],
                held.at[k, :, pl.ds(half * HALF, HALF)],
                sems.at[half, k],
            )
            for k, source in enumerate(sources)
        ]
        for half in range(2)
    ]


def experts(whole, copies, held, slot_weight, core, both):
    square = jnp.zeros((8, 128), F32)
    totals = [jnp.zeros((CAP, 128), F32) for _ in range(4)]
    for half in range(2):
        for copy in copies[half]:
            copy.wait()
        for at in range(half * HALF, (half + 1) * HALF, TILE):
            part = whole[at : at + TILE]
            values = part.astype(F32)
            square += jnp.sum((values * values).reshape(TILE // 8, 8, 128), axis=0)
            for k in range(4):
                totals[k] += jnp.dot(held[k, :, at : at + TILE], part, preferred_element_type=F32)
    scale = lax.rsqrt(jnp.sum(square, axis=0, keepdims=True) * (1.0 / D) + 1e-06)
    for k in range(2):
        first, second = totals[2 * k] * scale, totals[2 * k + 1] * scale
        at = pl.multiple_of((core if k == 0 else 1 - core) * CAP, 8)
        both[pl.ds(at, CAP), :] = first * (1.0 / (1.0 + jnp.exp(-first))) * second
    return both[...] * slot_weight


def first_kernel(place, *refs):
    pieces, weights = refs[:9], refs[9:13]
    slot_expert, out, current, slot_weight, rows, whole, both, held, sems = refs[13:]
    copies = weight_copies(weights, held, sems)
    for copy in copies[0] + copies[1]:
        copy.start()

    def body(chip, shard):
        rows[pl.ds(pl.multiple_of(chip * ROW_MAIN, 8), ROW_MAIN), :] = shard.astype(F32)

    each_shard(place, pieces, body)

    def turned(at):
        parts = [rows[pl.ds(at + step, CHIPS, stride=ROW_MAIN), :] for step in (0, CHUNKS, 2 * CHUNKS)]
        parts.append(jnp.zeros((TAIL, 128), F32))
        return jnp.concatenate(parts, axis=0).T

    for k in range(CHUNKS):
        whole[k * 128 : (k + 1) * 128, :] = turned(k).astype(BF)
    picks = [rows[pl.ds(OWN * CHUNKS + t, CHIPS, stride=ROW_MAIN), :] for t in range(OWN)]
    weight = jnp.concatenate(picks + [jnp.zeros((TAIL, 128), F32)], axis=0).T
    expert = slot_expert[...]
    slots = jnp.zeros((CHIP_CAP, 128), F32)
    for k in range(FLIGHT):
        slots += jnp.where(expert == k, weight[k : k + 1], 0.0)
    slot_weight[...] = slots
    at = pl.multiple_of((place[0] * NX + place[1]) * CHIP_FEAT, 16)
    current[...] = whole[pl.ds(at, CHIP_FEAT), :]
    hidden = experts(whole, copies, held, slots, place[2], both)
    out[...] = pack(hidden, HID_MAIN).astype(BF)


def gate_up_kernel(place, *refs):
    pieces, weights = refs[:9], refs[9:13]
    slot_weight, out, whole, both, held, sems = refs[13:]
    copies = weight_copies(weights, held, sems)
    for copy in copies[0] + copies[1]:
        copy.start()
    unpack(place, pieces, whole, CHIP_FEAT, ROW_MAIN)
    hidden = experts(whole, copies, held, slot_weight[...], place[2], both)
    out[...] = pack(hidden, HID_MAIN).astype(BF)


def update_kernel(place, *refs):
    pieces, picked = refs[:9], refs[9:11]
    current, out, packed, whole, both, held, sems = refs[11:]
    copies = [pltpu.make_async_copy(picked[k], held.at[k], sems.at[k]) for k in range(2)]
    for copy in copies:
        copy.start()
    unpack(place, pieces, whole, CHIP_CAP, HID_MAIN)
    for k, copy in enumerate(copies):
        copy.wait()
        total = jnp.zeros((FEAT, 128), F32)
        for at in range(0, CHIPS * CHIP_CAP, TILE):
            total += jnp.dot(
                held[k, :, at : at + TILE], whole[at : at + TILE], preferred_element_type=F32
            )
        at = pl.multiple_of((place[2] if k == 0 else 1 - place[2]) * FEAT, 8)
        both[pl.ds(at, FEAT), :] = total
    fresh = current[...].astype(F32) + both[...]
    out[...] = fresh.astype(BF)
    packed[...] = pack(fresh, ROW_MAIN).astype(BF)


def pick_kernel(replica, slot_units, b0, b1, b2, b3, out, slab):
    for by, block in zip((0, 1, 3, 2), (b0, b1, b2, b3)):
        at = lax.rem(replica[0] + NY - by, NY) * BLOCK
        slab[:, pl.ds(pl.multiple_of(at, BLOCK), BLOCK)] = block[...]

    def pair(p, carry):
        halves = []
        for side in range(2):
            start = slot_units[(2 * p + side) * CAP]
            base = jnp.minimum(start // 128, (UNITS - 384) // 128) * 128
            block = slab[:, pl.ds(pl.multiple_of(base, 128), 384)].astype(F32)
            halves.append(pltpu.roll(block, lax.rem(384 - (start - base), 384), 1)[:, :CAP])
        both = jnp.concatenate(halves, axis=1).astype(BF)
        out[:, pl.ds(pl.multiple_of(p * 384, 384), 384)] = both
        return carry

    lax.fori_loop(0, OWNERS // 2, pair, 0)


SMEM = pl.BlockSpec(memory_space=pltpu.SMEM)
VMEM = pl.BlockSpec(memory_space=pltpu.VMEM)
FAR = pl.BlockSpec(memory_space=pl.ANY)


def shape(*dims, dtype=BF):
    return jax.ShapeDtypeStruct(dims, dtype)


def call(kernel, outs, scratch, flops, moved_bytes, scalars, near, far=(), last=()):
    return pl.pallas_call(
        kernel,
        out_shape=outs,
        in_specs=[SMEM] * len(scalars) + [VMEM] * len(near) + [FAR] * len(far) + [VMEM] * len(last),
        out_specs=jax.tree.map(lambda _: VMEM, outs),
        scratch_shapes=scratch,
        compiler_params=pltpu.CompilerParams(vmem_limit_bytes=36 * 1024 * 1024),
        cost_estimate=pl.CostEstimate(flops=flops, bytes_accessed=moved_bytes, transcendentals=0),
    )(*scalars, *near, *far, *last)


GATE_SCRATCH = [
    pltpu.VMEM((D, 128), BF),
    pltpu.VMEM((CHIP_CAP, 128), F32),
    pltpu.VMEM((4, CAP, D), BF),
    pltpu.SemaphoreType.DMA((2, 4)),
]
UPDATE_SCRATCH = [
    pltpu.VMEM((CHIPS * CHIP_CAP, 128), BF),
    pltpu.VMEM((CHIP_FEAT, 128), F32),
    pltpu.VMEM((2, FEAT, CHIPS * CHIP_CAP), BF),
    pltpu.SemaphoreType.DMA((2,)),
]
GATE_FLOPS = 2 * 2 * CHIP_CAP * D * 128
UPDATE_FLOPS = 2 * CHIP_FEAT * CHIPS * CHIP_CAP * 128


def local(
    learner_hidden,
    learner_cot,
    master,
    moment_one,
    moment_two,
    slot_units,
    gate_slots,
    up_slots,
    norm_gain,
    tokens,
    routes,
    gate_weights,
):
    replica = lax.axis_index("dp")
    z, x, c = (lax.axis_index(axis) for axis in EXPERT)
    place = jnp.stack([z, x, c]).astype(jnp.int32)
    chip = z * NX + x

    expert_ids = jnp.arange(FLIGHT, dtype=jnp.int32)
    picks = (routes[:, :, None] == expert_ids[None, None, :]).astype(F32)
    weight = jnp.sum(gate_weights.astype(F32)[:, :, None] * picks, axis=1).astype(BF)
    below = jnp.pad(weight, ((0, ROW_MAIN - OWN * CHUNKS - OWN), (0, 128 - FLIGHT)))
    packed = jnp.concatenate([tokens.reshape(OWN * CHUNKS, 128), below], axis=0)

    grad = lax.dot_general(
        learner_hidden, learner_cot, (((0,), (0,)), ((), ())), preferred_element_type=F32
    )
    grad = grad.astype(BF)

    def block_for(by):
        return lax.dynamic_slice_in_dim(grad, (replica + by) % NY * BLOCK, BLOCK, 0)

    partial = [block_for(0)] + [send(block_for(by), "dp", NY, by) for by in (1, 3, 2)]
    grad = sum(part.astype(F32) for part in partial)
    moment_new = 0.9 * moment_one + 0.1 * grad
    second_new = 0.95 * moment_two + 0.05 * grad * grad
    corr_first = 1.0 - 0.9**ADAM_STEP
    corr_second = 1.0 - 0.95**ADAM_STEP
    master_new = master - 0.005 * (
        moment_new / corr_first / (jnp.sqrt(second_new / corr_second) + 1e-08) + 0.1 * master
    )
    slab = master_new.astype(BF).T

    pieces, gain, _ = gather_chips(packed, early=norm_gain)
    gain = gain.astype(F32)
    weights = [(slots.astype(F32) * gain).astype(BF) for slots in (gate_slots, up_slots)]
    weights += [send(own, "c", NC, 1) for own in weights]
    chip_slots = lax.dynamic_slice_in_dim(slot_units, chip * CHIP_CAP, CHIP_CAP)
    slot_expert = jnp.where(chip_slots < UNITS, chip_slots // FF, -1)[:, None]
    hidden, current, slot_weight = call(
        first_kernel,
        (shape(HID_MAIN, 128), shape(CHIP_FEAT, 128), shape(CHIP_CAP, 128, dtype=F32)),
        [pltpu.VMEM((CHIPS * ROW_MAIN, 128), F32)] + GATE_SCRATCH,
        GATE_FLOPS,
        13_000_000,
        [place], pieces, weights, [slot_expert],
    )
    hidden, slab = together(hidden, slab)
    blocks = [slab] + [send(slab, "dp", NY, by) for by in (1, 3, 2)]
    for step_index in range(STEPS):
        if step_index:
            pieces, _, _ = gather_chips(packed)
            hidden = call(
                gate_up_kernel,
                shape(HID_MAIN, 128),
                GATE_SCRATCH,
                GATE_FLOPS,
                13_000_000,
                [place], pieces, weights, [slot_weight],
            )
        pieces, _, listed = gather_chips(hidden, late=None if step_index else slot_units)
        if step_index == 0:
            own_picked = call(
                pick_kernel,
                shape(FEAT, OWNERS * CAP),
                [pltpu.VMEM((FEAT, UNITS), BF)],
                0,
                5_000_000,
                [replica.astype(jnp.int32)[None], listed], blocks,
            )
            picked = [own_picked, send(own_picked, "c", NC, 1)]
        current, packed = call(
            update_kernel,
            (shape(CHIP_FEAT, 128), shape(ROW_MAIN, 128)),
            UPDATE_SCRATCH,
            UPDATE_FLOPS,
            8_000_000,
            [place], pieces, picked, [current],
        )
    back = current[:, :ROWS].T.reshape(OWN, CHIPS, CHIP_FEAT).transpose(1, 0, 2)
    back = lax.all_to_all(back, ("z", "x"), split_axis=0, concat_axis=0, tiled=True)
    decoded = back.transpose(1, 0, 2).reshape(OWN, D)
    return (master_new, moment_new, second_new, decoded)


def solution(mesh):
    mesh = jax.sharding.Mesh(mesh.devices.reshape(NY, NZ, NX, NC), ("dp",) + EXPERT)
    placed = (
        P("dp", None),
        P("dp", EXPERT),
        P("dp", EXPERT),
        P("dp", EXPERT),
        P("dp", EXPERT),
        P(),
        P(EXPERT, None),
        P(EXPERT, None),
        P(),
        P(("dp",) + EXPERT, None),
        P(("dp",) + EXPERT, None),
        P(("dp",) + EXPERT, None),
    )
    return jax.shard_map(
        local,
        mesh=mesh,
        in_specs=placed,
        out_specs=(
            P("dp", EXPERT),
            P("dp", EXPERT),
            P("dp", EXPERT),
            P(("dp",) + EXPERT, None),
        ),
        check_vma=False,
    )
```

```python
import jax
import jax.numpy as jnp
from jax import lax
from jax.experimental import pallas as pl
from jax.experimental.pallas import tpu as pltpu
from jax.sharding import PartitionSpec as P

D = 7168
FF = 2048
STEPS = 2
ADAM_STEP = 10
UNITS = 8192
FLIGHT = 4
CAP = 192
OWNERS = 64
NZ, NX, NC, NY = 8, 4, 2, 4
CHIPS = NZ * NX
FEAT = D // OWNERS
CHIP_FEAT = D // CHIPS
CHIP_CAP = NC * CAP
BLOCK = UNITS // NY
OWN = 3
ROWS = OWN * CHIPS
TAIL = 128 - ROWS
ROW_MAIN = 176
HID_MAIN = 288
CHUNKS = D // 128
X_ORDER = (0, 3, 1, 2)
TILE = 512
EXPERT = ("z", "x", "c")
Z_ORDER = (0, 7, 1, 6, 2, 5, 3, 4, 4)
BF = jnp.bfloat16
F32 = jnp.float32


def send(value, axis, size, by):
    return lax.ppermute(value, axis, [(i, (i + by) % size) for i in range(size)])


def together(*values):
    return lax.optimization_barrier(values)


def gather_chips(shard, ties=()):
    four = jnp.stack([shard] + [send(shard, "x", NX, by) for by in (1, 3, 2)])
    pieces, up, down = [four], four, four
    tied = ()
    for step in range(3):
        up, down = send(up, "z", NZ, 1), send(down, "z", NZ, -1)
        if ties and step == ties[0]:
            up, down, *tied = together(up, down, *ties[1])
        pieces += [up, down]
    return pieces + [send(up[:2], "z", NZ, 1), send(down[2:], "z", NZ, -1)], tied


def each_shard(place, pieces, body):
    for i, piece in enumerate(pieces):
        plane = lax.rem(place[0] + Z_ORDER[i], NZ) * NX
        for j in range(piece.shape[0]):
            x = lax.rem(place[1] + X_ORDER[j + (2 if i == 8 else 0)], NX)
            body(plane + x, piece[j])


def pack(full, main, extra=()):
    parts = [full[main:, k : k + TAIL] for k in range(0, ROWS, TAIL)]
    parts += [row[:, k : k + TAIL] for row in extra for k in range(0, ROWS, TAIL)]
    missing = main - sum(part.shape[0] for part in parts)
    if missing:
        parts.append(jnp.zeros((missing, TAIL), full.dtype))
    return jnp.concatenate([full[:main, :ROWS], jnp.concatenate(parts, axis=0)], axis=1)


def unpack(place, pieces, whole, size, main, extra=None):
    rest = size - main
    if extra is not None:
        extra[...] = jnp.zeros(extra.shape, F32)

    def body(chip, shard):
        at = pl.multiple_of(chip * size, 16)
        whole[pl.ds(at, main), :] = shard
        parts = [shard[k * rest : (k + 1) * rest, ROWS:] for k in range(3)]
        whole[pl.ds(pl.multiple_of(at + main, 16), rest), :] = jnp.concatenate(
            parts + parts[:1], axis=1
        )
        if extra is not None:
            extra[...] += shard[3 * rest : 3 * rest + 16].astype(F32)

    each_shard(place, pieces, body)


HALF = D // 2


def weight_copies(sources, held, sems):
    return [
        [
            pltpu.make_async_copy(
                source.at[:, pl.ds(half * HALF, HALF)],
                held.at[k, :, pl.ds(half * HALF, HALF)],
                sems.at[half, k],
            )
            for k, source in enumerate(sources)
        ]
        for half in range(2)
    ]


def experts(whole, square, copies, held, slot_weight, core, both):
    totals = [jnp.zeros((CAP, 128), F32) for _ in range(4)]
    for half in range(2):
        for copy in copies[half]:
            copy.wait()
        for at in range(half * HALF, (half + 1) * HALF, TILE):
            part = whole[at : at + TILE]
            for k in range(4):
                totals[k] += jnp.dot(held[k, :, at : at + TILE], part, preferred_element_type=F32)
    scale = lax.rsqrt(square * (1.0 / D) + 1e-06)
    for k in range(2):
        first, second = totals[2 * k] * scale, totals[2 * k + 1] * scale
        at = pl.multiple_of((core if k == 0 else 1 - core) * CAP, 8)
        both[pl.ds(at, CAP), :] = first * (1.0 / (1.0 + jnp.exp(-first))) * second
    return both[...] * slot_weight


def first_kernel(place, *refs):
    pieces, weights = refs[:9], refs[9:13]
    slot_expert, gain, out, current, slot_weight, rows, turn, whole, both, held, sems = refs[13:]
    copies = weight_copies(weights, held, sems)
    for copy in copies[0] + copies[1]:
        copy.start()

    def body(chip, shard):
        rows[pl.ds(pl.multiple_of(chip * ROW_MAIN, 8), ROW_MAIN), :] = shard.astype(F32)

    each_shard(place, pieces, body)

    def chunk(at):
        parts = [rows[pl.ds(at + step, CHIPS, stride=ROW_MAIN), :] for step in (0, CHUNKS, 2 * CHUNKS)]
        parts.append(jnp.zeros((TAIL, 128), F32))
        return jnp.concatenate(parts, axis=0)

    square = jnp.zeros((128, 128), F32)
    for k in range(CHUNKS):
        values = chunk(k)
        square += values * values
        whole[k * 128 : (k + 1) * 128, :] = (values * gain[k : k + 1, :]).T.astype(BF)
    square = jnp.sum(square.T, axis=0, keepdims=True)
    picks = [rows[pl.ds(OWN * CHUNKS + t, CHIPS, stride=ROW_MAIN), :] for t in range(OWN)]
    weight = jnp.concatenate(picks + [jnp.zeros((TAIL, 128), F32)], axis=0).T
    expert = slot_expert[...]
    slots = jnp.zeros((CHIP_CAP, 128), F32)
    for k in range(FLIGHT):
        slots += jnp.where(expert == k, weight[k : k + 1], 0.0)
    slot_weight[...] = slots
    at = (place[0] * NX + place[1]) * CHIP_FEAT
    base = jnp.minimum(at // 128, CHUNKS - 3)
    for k in range(3):
        turn[k * 128 : (k + 1) * 128, :] = chunk(base + k).T
    current[...] = turn[pl.ds(pl.multiple_of(at - base * 128, 8), CHIP_FEAT), :].astype(BF)
    hidden = experts(whole, square, copies, held, slots, place[2], both)
    out[...] = pack(hidden, HID_MAIN).astype(BF)


def gate_up_kernel(place, *refs):
    pieces, weights = refs[:9], refs[9:13]
    slot_weight, out, extra, whole, both, held, sems = refs[13:]
    copies = weight_copies(weights, held, sems)
    for copy in copies[0] + copies[1]:
        copy.start()
    unpack(place, pieces, whole, CHIP_FEAT, ROW_MAIN, extra)
    sums = extra[0:3, ROWS:] + extra[3:6, ROWS:]
    square = jnp.concatenate([sums[0:1], sums[1:2], sums[2:3], sums[0:1]], axis=1)
    hidden = experts(whole, square, copies, held, slot_weight[...], place[2], both)
    out[...] = pack(hidden, HID_MAIN).astype(BF)


def update_kernel(place, *refs):
    pieces, picked = refs[:9], refs[9:11]
    current, gain, out, packed, whole, both, held, sems = refs[11:]
    copies = [pltpu.make_async_copy(picked[k], held.at[k], sems.at[k]) for k in range(2)]
    for copy in copies:
        copy.start()
    unpack(place, pieces, whole, CHIP_CAP, HID_MAIN)
    for k, copy in enumerate(copies):
        copy.wait()
        total = jnp.zeros((FEAT, 128), F32)
        for at in range(0, CHIPS * CHIP_CAP, TILE):
            total += jnp.dot(
                held[k, :, at : at + TILE], whole[at : at + TILE], preferred_element_type=F32
            )
        at = pl.multiple_of((place[2] if k == 0 else 1 - place[2]) * FEAT, 8)
        both[pl.ds(at, FEAT), :] = total
    fresh = (current[...].astype(F32) + both[...]).astype(BF)
    out[...] = fresh
    fresh = fresh.astype(F32)
    square = jnp.sum(fresh * fresh, axis=0, keepdims=True)
    high = square.astype(BF).astype(F32)
    packed[...] = pack(fresh * gain[...], ROW_MAIN, (high, square - high)).astype(BF)


def pick_kernel(replica, slot_units, b0, b1, b2, b3, out, slab):
    for by, block in zip((0, 1, 3, 2), (b0, b1, b2, b3)):
        at = lax.rem(replica[0] + NY - by, NY) * BLOCK
        slab[:, pl.ds(pl.multiple_of(at, BLOCK), BLOCK)] = block[...]
    slab[:, UNITS:] = jnp.zeros((FEAT, 256), BF)
    lane = lax.broadcasted_iota(jnp.int32, (FEAT, 128), 1)

    def window(owner, lead):
        start = slot_units[owner * CAP]
        base = start // 128
        off = start - base * 128
        tiles = []
        for k in range(3):
            tile = slab[:, pl.ds(pl.multiple_of((base + k) * 128, 128), 128)].astype(F32)
            tiles.append(pltpu.roll(tile, lax.rem(128 - off + lead, 128), 1))
        return off, tiles

    def pair(p, carry):
        off, (r0, r1, r2) = window(2 * p, 0)
        out0 = jnp.where(lane < 128 - off, r0, r1)
        out1 = jnp.where(lane < 128 - off, r1, r2)
        off, (r0, r1, r2) = window(2 * p + 1, 64)
        late = jnp.where(lane < 192 - off, r0, r1)
        out2 = jnp.where(lane < 64 - off, r0, jnp.where(lane < 192 - off, r1, r2))
        out1 = jnp.where(lane < 64, out1, late)
        both = jnp.concatenate([out0, out1, out2], axis=1).astype(BF)
        out[:, pl.ds(pl.multiple_of(p * 384, 384), 384)] = both
        return carry

    lax.fori_loop(0, OWNERS // 2, pair, 0)


SMEM = pl.BlockSpec(memory_space=pltpu.SMEM)
VMEM = pl.BlockSpec(memory_space=pltpu.VMEM)
FAR = pl.BlockSpec(memory_space=pl.ANY)


def shape(*dims, dtype=BF):
    return jax.ShapeDtypeStruct(dims, dtype)


def call(kernel, outs, scratch, flops, moved_bytes, scalars, near, far=(), last=()):
    return pl.pallas_call(
        kernel,
        out_shape=outs,
        in_specs=[SMEM] * len(scalars) + [VMEM] * len(near) + [FAR] * len(far) + [VMEM] * len(last),
        out_specs=jax.tree.map(lambda _: VMEM, outs),
        scratch_shapes=scratch,
        compiler_params=pltpu.CompilerParams(vmem_limit_bytes=36 * 1024 * 1024),
        cost_estimate=pl.CostEstimate(flops=flops, bytes_accessed=moved_bytes, transcendentals=0),
    )(*scalars, *near, *far, *last)


GATE_SCRATCH = [
    pltpu.VMEM((D, 128), BF),
    pltpu.VMEM((CHIP_CAP, 128), F32),
    pltpu.VMEM((4, CAP, D), BF),
    pltpu.SemaphoreType.DMA((2, 4)),
]
UPDATE_SCRATCH = [
    pltpu.VMEM((CHIPS * CHIP_CAP, 128), BF),
    pltpu.VMEM((CHIP_FEAT, 128), F32),
    pltpu.VMEM((2, FEAT, CHIPS * CHIP_CAP), BF),
    pltpu.SemaphoreType.DMA((2,)),
]
GATE_FLOPS = 2 * 2 * CHIP_CAP * D * 128
UPDATE_FLOPS = 2 * CHIP_FEAT * CHIPS * CHIP_CAP * 128


def local(
    learner_hidden,
    learner_cot,
    master,
    moment_one,
    moment_two,
    slot_units,
    gate_slots,
    up_slots,
    norm_gain,
    tokens,
    routes,
    gate_weights,
):
    replica = lax.axis_index("dp")
    z, x, c = (lax.axis_index(axis) for axis in EXPERT)
    place = jnp.stack([z, x, c]).astype(jnp.int32)
    chip = z * NX + x

    expert_ids = jnp.arange(FLIGHT, dtype=jnp.int32)
    picks = (routes[:, :, None] == expert_ids[None, None, :]).astype(F32)
    weight = jnp.sum(gate_weights.astype(F32)[:, :, None] * picks, axis=1).astype(BF)
    below = jnp.pad(weight, ((0, ROW_MAIN - OWN * CHUNKS - OWN), (0, 128 - FLIGHT)))
    packed = jnp.concatenate([tokens.reshape(OWN * CHUNKS, 128), below], axis=0)

    grad = lax.dot_general(
        learner_hidden, learner_cot, (((0,), (0,)), ((), ())), preferred_element_type=F32
    )
    grad = grad.astype(BF)

    def block_for(by):
        return lax.dynamic_slice_in_dim(grad, (replica + by) % NY * BLOCK, BLOCK, 0)

    outgoing = [block_for(by) for by in (1, 3, 2)]
    packed, *outgoing = together(packed, *outgoing)
    arriving = [send(block, "dp", NY, by) for block, by in zip(outgoing, (1, 3, 2))]
    pieces, arriving = gather_chips(packed, (1, arriving))
    grad = sum(part.astype(F32) for part in [block_for(0), *arriving])
    moment_new = 0.9 * moment_one + 0.1 * grad
    second_new = 0.95 * moment_two + 0.05 * grad * grad
    corr_first = 1.0 - 0.9**ADAM_STEP
    corr_second = 1.0 - 0.95**ADAM_STEP
    master_new = master - 0.005 * (
        moment_new / corr_first / (jnp.sqrt(second_new / corr_second) + 1e-08) + 0.1 * master
    )
    slab = master_new.astype(BF).T

    weights = [gate_slots, up_slots] + [send(own, "c", NC, 1) for own in (gate_slots, up_slots)]
    gain = norm_gain.astype(F32)
    chip_gain = lax.dynamic_slice_in_dim(gain, chip * CHIP_FEAT, CHIP_FEAT)[:, None]
    chip_slots = lax.dynamic_slice_in_dim(slot_units, chip * CHIP_CAP, CHIP_CAP)
    slot_expert = jnp.where(chip_slots < UNITS, chip_slots // FF, -1)[:, None]
    hidden, current, slot_weight = call(
        first_kernel,
        (shape(HID_MAIN, 128), shape(CHIP_FEAT, 128), shape(CHIP_CAP, 128, dtype=F32)),
        [pltpu.VMEM((CHIPS * ROW_MAIN, 128), F32), pltpu.VMEM((384, 128), F32)] + GATE_SCRATCH,
        GATE_FLOPS,
        13_000_000,
        [place], pieces, weights, [slot_expert, gain.reshape(CHUNKS, 128)],
    )
    hidden, slab = together(hidden, slab)
    blocks = [slab] + [send(slab, "dp", NY, by) for by in (1, 3, 2)]
    for step_index in range(STEPS):
        if step_index:
            pieces, _ = gather_chips(packed)
            hidden = call(
                gate_up_kernel,
                shape(HID_MAIN, 128),
                [pltpu.VMEM((16, 128), F32)] + GATE_SCRATCH,
                GATE_FLOPS,
                13_000_000,
                [place], pieces, weights, [slot_weight],
            )
        pieces, tied = gather_chips(hidden, () if step_index else (1, [slot_units]))
        if step_index == 0:
            own_picked = call(
                pick_kernel,
                shape(FEAT, OWNERS * CAP),
                [pltpu.VMEM((FEAT, UNITS + 256), BF)],
                0,
                5_000_000,
                [replica.astype(jnp.int32)[None], *tied], blocks,
            )
            picked = [own_picked, send(own_picked, "c", NC, 1)]
        current, packed = call(
            update_kernel,
            (shape(CHIP_FEAT, 128), shape(ROW_MAIN, 128)),
            UPDATE_SCRATCH,
            UPDATE_FLOPS,
            8_000_000,
            [place], pieces, picked, [current, chip_gain],
        )
    back = current[:, :ROWS].T.reshape(OWN, CHIPS, CHIP_FEAT).transpose(1, 0, 2)
    back = lax.all_to_all(back, ("z", "x"), split_axis=0, concat_axis=0, tiled=True)
    decoded = back.transpose(1, 0, 2).reshape(OWN, D)
    return (master_new, moment_new, second_new, decoded)


def solution(mesh):
    mesh = jax.sharding.Mesh(mesh.devices.reshape(NY, NZ, NX, NC), ("dp",) + EXPERT)
    placed = (
        P("dp", None),
        P("dp", EXPERT),
        P("dp", EXPERT),
        P("dp", EXPERT),
        P("dp", EXPERT),
        P(),
        P(EXPERT, None),
        P(EXPERT, None),
        P(),
        P(("dp",) + EXPERT, None),
        P(("dp",) + EXPERT, None),
        P(("dp",) + EXPERT, None),
    )
    return jax.shard_map(
        local,
        mesh=mesh,
        in_specs=placed,
        out_specs=(
            P("dp", EXPERT),
            P("dp", EXPERT),
            P("dp", EXPERT),
            P(("dp",) + EXPERT, None),
        ),
        check_vma=False,
    )
```

```python
import jax
import jax.numpy as jnp
from jax import lax
from jax.experimental import pallas as pl
from jax.experimental.pallas import tpu as pltpu
from jax.sharding import PartitionSpec as P

D = 7168
FF = 2048
STEPS = 2
ADAM_STEP = 10
UNITS = 8192
FLIGHT = 4
CAP = 192
OWNERS = 64
NZ, NX, NC, NY = 8, 4, 2, 4
CHIPS = NZ * NX
FEAT = D // OWNERS
CHIP_FEAT = D // CHIPS
CHIP_CAP = NC * CAP
BLOCK = UNITS // NY
OWN = 3
ROWS = OWN * CHIPS
TAIL = 128 - ROWS
ROW_MAIN = 176
HID_MAIN = 288
CHUNKS = D // 128
PLANE_FEAT = NX * CHIP_FEAT
PLANE_CAP = NX * CHIP_CAP
X_ORDER = (0, 3, 1, 2)
TILE = 512
EXPERT = ("z", "x", "c")
Z_ORDER = (0, 7, 1, 6, 2, 5, 3, 4, 4)
BF = jnp.bfloat16
F32 = jnp.float32


def send(value, axis, size, by):
    return lax.ppermute(value, axis, [(i, (i + by) % size) for i in range(size)])


def together(*values):
    return lax.optimization_barrier(values)


def gather_chips(shard, ties=()):
    four = jnp.stack([shard] + [send(shard, "x", NX, by) for by in (1, 3, 2)])
    tied = []
    if ties:
        four, first = together(four, ties[0])
        tied.append(first)
    pieces, up, down = [four], four, four
    for step in range(3):
        up, down = send(up, "z", NZ, 1), send(down, "z", NZ, -1)
        if step + 1 < len(ties):
            up, down, one = together(up, down, ties[step + 1])
            tied.append(one)
        pieces += [up, down]
    return pieces + [send(up[:2], "z", NZ, 1), send(down[2:], "z", NZ, -1)], tied


def each_shard(place, pieces, body):
    for i, piece in enumerate(pieces):
        plane = lax.rem(place[0] + Z_ORDER[i], NZ) * NX
        for j in range(piece.shape[0]):
            x = lax.rem(place[1] + X_ORDER[j + (2 if i == 8 else 0)], NX)
            body(plane + x, piece[j])


def pack(full, main, extra=()):
    parts = [full[main:, k : k + TAIL] for k in range(0, ROWS, TAIL)]
    parts += [row[:, k : k + TAIL] for row in extra for k in range(0, ROWS, TAIL)]
    missing = main - sum(part.shape[0] for part in parts)
    if missing:
        parts.append(jnp.zeros((missing, TAIL), full.dtype))
    return jnp.concatenate([full[:main, :ROWS], jnp.concatenate(parts, axis=0)], axis=1)


def unpack(place, piece, first, plane, size, main, extra=None):
    rest = size - main
    for j in range(piece.shape[0]):
        shard = piece[j]
        at = pl.multiple_of(lax.rem(place[1] + X_ORDER[first + j], NX) * size, 16)
        plane[pl.ds(at, main), :] = shard[:main]
        parts = [shard[k * rest : (k + 1) * rest, ROWS:] for k in range(3)]
        plane[pl.ds(pl.multiple_of(at + main, 16), rest), :] = jnp.concatenate(
            parts + parts[:1], axis=1
        )
        if extra is not None:
            extra[...] += shard[3 * rest : 3 * rest + 16].astype(F32)


def plane_copies(place, planes, width, sources, held, sems):
    copies = []
    for i, plane in enumerate(planes):
        at = pl.multiple_of(lax.rem(place[0] + Z_ORDER[plane], NZ) * width, 128)
        copies.append([
            pltpu.make_async_copy(source.at[:, pl.ds(at, width)], held.at[i, k], sems.at[i, k])
            for k, source in enumerate(sources)
        ])
    for row in copies:
        for copy in row:
            copy.start()
    return copies


HALF = D // 2


def weight_copies(sources, held, sems):
    return [
        [
            pltpu.make_async_copy(
                source.at[:, pl.ds(half * HALF, HALF)],
                held.at[k, :, pl.ds(half * HALF, HALF)],
                sems.at[half, k],
            )
            for k, source in enumerate(sources)
        ]
        for half in range(2)
    ]


def experts(whole, square, copies, held, slot_weight, core, both):
    totals = [jnp.zeros((CAP, 128), F32) for _ in range(4)]
    for half in range(2):
        for copy in copies[half]:
            copy.wait()
        for at in range(half * HALF, (half + 1) * HALF, TILE):
            part = whole[at : at + TILE]
            for k in range(4):
                totals[k] += jnp.dot(held[k, :, at : at + TILE], part, preferred_element_type=F32)
    return activated(totals, square, slot_weight, core, both)


def activated(totals, square, slot_weight, core, both):
    scale = lax.rsqrt(square * (1.0 / D) + 1e-06)
    for k in range(2):
        first, second = totals[2 * k] * scale, totals[2 * k + 1] * scale
        at = pl.multiple_of((core if k == 0 else 1 - core) * CAP, 8)
        both[pl.ds(at, CAP), :] = first * (1.0 / (1.0 + jnp.exp(-first))) * second
    return both[...] * slot_weight


def first_kernel(place, *refs):
    pieces, weights = refs[:9], refs[9:13]
    slot_expert, gain, out, current, slot_weight, rows, turn, whole, both, held, sems = refs[13:]
    copies = weight_copies(weights, held, sems)
    for copy in copies[0] + copies[1]:
        copy.start()

    def body(chip, shard):
        rows[pl.ds(pl.multiple_of(chip * ROW_MAIN, 8), ROW_MAIN), :] = shard.astype(F32)

    each_shard(place, pieces, body)

    def chunk(at):
        parts = [rows[pl.ds(at + step, CHIPS, stride=ROW_MAIN), :] for step in (0, CHUNKS, 2 * CHUNKS)]
        parts.append(jnp.zeros((TAIL, 128), F32))
        return jnp.concatenate(parts, axis=0)

    square = jnp.zeros((128, 128), F32)
    for k in range(CHUNKS):
        values = chunk(k)
        square += values * values
        whole[k * 128 : (k + 1) * 128, :] = (values * gain[k : k + 1, :]).T.astype(BF)
    square = jnp.sum(square.T, axis=0, keepdims=True)
    picks = [rows[pl.ds(OWN * CHUNKS + t, CHIPS, stride=ROW_MAIN), :] for t in range(OWN)]
    weight = jnp.concatenate(picks + [jnp.zeros((TAIL, 128), F32)], axis=0).T
    expert = slot_expert[...]
    slots = jnp.zeros((CHIP_CAP, 128), F32)
    for k in range(FLIGHT):
        slots += jnp.where(expert == k, weight[k : k + 1], 0.0)
    slot_weight[...] = slots
    at = (place[0] * NX + place[1]) * CHIP_FEAT
    base = jnp.minimum(at // 128, CHUNKS - 3)
    for k in range(3):
        turn[k * 128 : (k + 1) * 128, :] = chunk(base + k).T
    current[...] = turn[pl.ds(pl.multiple_of(at - base * 128, 8), CHIP_FEAT), :].astype(BF)
    hidden = experts(whole, square, copies, held, slots, place[2], both)
    out[...] = pack(hidden, HID_MAIN).astype(BF)


def gate_up_kernel(place, *refs):
    pieces, weights = refs[:7], refs[7:11]
    out, extra, planes, held, sems = refs[11:]
    copies = plane_copies(place, range(7), PLANE_FEAT, weights, held, sems)
    extra[...] = jnp.zeros(extra.shape, F32)
    totals = [jnp.zeros((CAP, 128), F32) for _ in range(4)]
    for i in range(7):
        unpack(place, pieces[i], 0, planes.at[i], CHIP_FEAT, ROW_MAIN, extra)
        for k in range(4):
            copies[i][k].wait()
            totals[k] += jnp.dot(held[i, k], planes[i], preferred_element_type=F32)
    for k in range(4):
        out[k] = totals[k]


def gate_up_last_kernel(place, *refs):
    pieces, weights = refs[:2], refs[2:6]
    before, extra_before, slot_weight, out, extra, both, plane, held, sems = refs[6:]
    copies = plane_copies(place, (7,), PLANE_FEAT, weights, held, sems)
    extra[...] = extra_before[...]
    for i in range(2):
        unpack(place, pieces[i], 2 * i, plane, CHIP_FEAT, ROW_MAIN, extra)
    totals = []
    for k in range(4):
        copies[0][k].wait()
        totals.append(before[k] + jnp.dot(held[0, k], plane[...], preferred_element_type=F32))
    sums = extra[0:3, ROWS:] + extra[3:6, ROWS:]
    square = jnp.concatenate([sums[0:1], sums[1:2], sums[2:3], sums[0:1]], axis=1)
    hidden = activated(totals, square, slot_weight[...], place[2], both)
    out[...] = pack(hidden, HID_MAIN).astype(BF)


def update_kernel(place, *refs):
    pieces, picked = refs[:7], refs[7:9]
    out, planes, held, sems = refs[9:]
    copies = plane_copies(place, range(7), PLANE_CAP, picked, held, sems)
    totals = [jnp.zeros((FEAT, 128), F32) for _ in range(2)]
    for i in range(7):
        unpack(place, pieces[i], 0, planes.at[i], CHIP_CAP, HID_MAIN)
        for k in range(2):
            copies[i][k].wait()
            totals[k] += jnp.dot(held[i, k], planes[i], preferred_element_type=F32)
    for k in range(2):
        out[k] = totals[k]


def update_last_kernel(place, *refs):
    pieces, picked = refs[:2], refs[2:4]
    before, current, gain, out, packed, both, plane, held, sems = refs[4:]
    copies = plane_copies(place, (7,), PLANE_CAP, picked, held, sems)
    for i in range(2):
        unpack(place, pieces[i], 2 * i, plane, CHIP_CAP, HID_MAIN)
    for k in range(2):
        copies[0][k].wait()
        total = before[k] + jnp.dot(held[0, k], plane[...], preferred_element_type=F32)
        at = pl.multiple_of((place[2] if k == 0 else 1 - place[2]) * FEAT, 8)
        both[pl.ds(at, FEAT), :] = total
    fresh = (current[...].astype(F32) + both[...]).astype(BF)
    out[...] = fresh
    fresh = fresh.astype(F32)
    square = jnp.sum(fresh * fresh, axis=0, keepdims=True)
    high = square.astype(BF).astype(F32)
    packed[...] = pack(fresh * gain[...], ROW_MAIN, (high, square - high)).astype(BF)


def pick_kernel(replica, slot_units, b0, b1, b2, b3, out, slab):
    for by, block in zip((0, 1, 3, 2), (b0, b1, b2, b3)):
        at = lax.rem(replica[0] + NY - by, NY) * BLOCK
        slab[:, pl.ds(pl.multiple_of(at, BLOCK), BLOCK)] = block[...]
    slab[:, UNITS:] = jnp.zeros((FEAT, 256), BF)
    lane = lax.broadcasted_iota(jnp.int32, (FEAT, 128), 1)

    def window(owner, lead):
        start = slot_units[owner * CAP]
        base = start // 128
        off = start - base * 128
        tiles = []
        for k in range(3):
            tile = slab[:, pl.ds(pl.multiple_of((base + k) * 128, 128), 128)].astype(F32)
            tiles.append(pltpu.roll(tile, lax.rem(128 - off + lead, 128), 1))
        return off, tiles

    def pair(p, carry):
        off, (r0, r1, r2) = window(2 * p, 0)
        out0 = jnp.where(lane < 128 - off, r0, r1)
        out1 = jnp.where(lane < 128 - off, r1, r2)
        off, (r0, r1, r2) = window(2 * p + 1, 64)
        late = jnp.where(lane < 192 - off, r0, r1)
        out2 = jnp.where(lane < 64 - off, r0, jnp.where(lane < 192 - off, r1, r2))
        out1 = jnp.where(lane < 64, out1, late)
        both = jnp.concatenate([out0, out1, out2], axis=1).astype(BF)
        out[:, pl.ds(pl.multiple_of(p * 384, 384), 384)] = both
        return carry

    lax.fori_loop(0, OWNERS // 2, pair, 0)


SMEM = pl.BlockSpec(memory_space=pltpu.SMEM)
VMEM = pl.BlockSpec(memory_space=pltpu.VMEM)
FAR = pl.BlockSpec(memory_space=pl.ANY)


def shape(*dims, dtype=BF):
    return jax.ShapeDtypeStruct(dims, dtype)


def call(kernel, outs, scratch, vmem, flops, moved_bytes, scalars, near, far=(), last=()):
    return pl.pallas_call(
        kernel,
        out_shape=outs,
        in_specs=[SMEM] * len(scalars) + [VMEM] * len(near) + [FAR] * len(far) + [VMEM] * len(last),
        out_specs=jax.tree.map(lambda _: VMEM, outs),
        scratch_shapes=scratch,
        compiler_params=pltpu.CompilerParams(vmem_limit_bytes=vmem * 1024 * 1024),
        cost_estimate=pl.CostEstimate(flops=flops, bytes_accessed=moved_bytes, transcendentals=0),
    )(*scalars, *near, *far, *last)


GATE_SCRATCH = [
    pltpu.VMEM((D, 128), BF),
    pltpu.VMEM((CHIP_CAP, 128), F32),
    pltpu.VMEM((4, CAP, D), BF),
    pltpu.SemaphoreType.DMA((2, 4)),
]


def plane_scratch(planes, width, sources, rows):
    lead = (planes,) if planes > 1 else ()
    return [
        pltpu.VMEM(lead + (width, 128), BF),
        pltpu.VMEM((planes, sources, rows, width), BF),
        pltpu.SemaphoreType.DMA((planes, sources)),
    ]


GATE_FLOPS = 2 * 2 * CHIP_CAP * D * 128
UPDATE_FLOPS = 2 * CHIP_FEAT * CHIPS * CHIP_CAP * 128


def local(
    learner_hidden,
    learner_cot,
    master,
    moment_one,
    moment_two,
    slot_units,
    gate_slots,
    up_slots,
    norm_gain,
    tokens,
    routes,
    gate_weights,
):
    replica = lax.axis_index("dp")
    z, x, c = (lax.axis_index(axis) for axis in EXPERT)
    place = jnp.stack([z, x, c]).astype(jnp.int32)
    chip = z * NX + x

    expert_ids = jnp.arange(FLIGHT, dtype=jnp.int32)
    picks = (routes[:, :, None] == expert_ids[None, None, :]).astype(F32)
    weight = jnp.sum(gate_weights.astype(F32)[:, :, None] * picks, axis=1).astype(BF)
    below = jnp.pad(weight, ((0, ROW_MAIN - OWN * CHUNKS - OWN), (0, 128 - FLIGHT)))
    packed = jnp.concatenate([tokens.reshape(OWN * CHUNKS, 128), below], axis=0)

    grad = lax.dot_general(
        learner_hidden, learner_cot, (((0,), (0,)), ((), ())), preferred_element_type=F32
    )
    grad = grad.astype(BF)

    def block_for(by):
        return lax.dynamic_slice_in_dim(grad, (replica + by) % NY * BLOCK, BLOCK, 0)

    outgoing = [block_for(by) for by in (1, 3, 2)]
    packed, *outgoing = together(packed, *outgoing)
    arriving = [send(block, "dp", NY, by) for block, by in zip(outgoing, (1, 3, 2))]
    pieces, arriving = gather_chips(packed, arriving)
    grad = sum(part.astype(F32) for part in [block_for(0), *arriving])
    moment_new = 0.9 * moment_one + 0.1 * grad
    second_new = 0.95 * moment_two + 0.05 * grad * grad
    corr_first = 1.0 - 0.9**ADAM_STEP
    corr_second = 1.0 - 0.95**ADAM_STEP
    master_new = master - 0.005 * (
        moment_new / corr_first / (jnp.sqrt(second_new / corr_second) + 1e-08) + 0.1 * master
    )
    slab = master_new.astype(BF).T

    weights = [gate_slots, up_slots] + [send(own, "c", NC, 1) for own in (gate_slots, up_slots)]
    gain = norm_gain.astype(F32)
    chip_gain = lax.dynamic_slice_in_dim(gain, chip * CHIP_FEAT, CHIP_FEAT)[:, None]
    chip_slots = lax.dynamic_slice_in_dim(slot_units, chip * CHIP_CAP, CHIP_CAP)
    slot_expert = jnp.where(chip_slots < UNITS, chip_slots // FF, -1)[:, None]
    hidden, current, slot_weight = call(
        first_kernel,
        (shape(HID_MAIN, 128), shape(CHIP_FEAT, 128), shape(CHIP_CAP, 128, dtype=F32)),
        [pltpu.VMEM((CHIPS * ROW_MAIN, 128), F32), pltpu.VMEM((384, 128), F32)] + GATE_SCRATCH,
        28,
        GATE_FLOPS,
        13_000_000,
        [place], pieces, weights, [slot_expert, gain.reshape(CHUNKS, 128)],
    )
    hidden, slab = together(hidden, slab)
    blocks = [send(slab, "dp", NY, by) for by in (1, 3, 2)]
    for step_index in range(STEPS):
        if step_index:
            pieces, _ = gather_chips(packed)
            before, extra = call(
                gate_up_kernel,
                (shape(4, CAP, 128, dtype=F32), shape(16, 128, dtype=F32)),
                plane_scratch(7, PLANE_FEAT, 4, CAP),
                24,
                GATE_FLOPS * 7 // 8,
                10_000_000,
                [place], pieces[:7], weights,
            )
            hidden = call(
                gate_up_last_kernel,
                shape(HID_MAIN, 128),
                [pltpu.VMEM((16, 128), F32), pltpu.VMEM((CHIP_CAP, 128), F32)]
                + plane_scratch(1, PLANE_FEAT, 4, CAP),
                8,
                GATE_FLOPS // 8,
                2_000_000,
                [place], pieces[7:], weights, [before, extra, slot_weight],
            )
        pieces, tied = gather_chips(hidden, () if step_index else blocks)
        if step_index == 0:
            own_picked = call(
                pick_kernel,
                shape(FEAT, OWNERS * CAP),
                [pltpu.VMEM((FEAT, UNITS + 256), BF)],
                14,
                0,
                5_000_000,
                [lax.axis_index("dp").astype(jnp.int32)[None], slot_units], [slab, *tied],
            )
            picked = [own_picked, send(own_picked, "c", NC, 1)]
        before = call(
            update_kernel,
            shape(2, FEAT, 128, dtype=F32),
            plane_scratch(7, PLANE_CAP, 2, FEAT),
            18,
            UPDATE_FLOPS * 7 // 8,
            7_000_000,
            [place], pieces[:7], picked,
        )
        current, packed = call(
            update_last_kernel,
            (shape(CHIP_FEAT, 128), shape(ROW_MAIN, 128)),
            [pltpu.VMEM((CHIP_FEAT, 128), F32)] + plane_scratch(1, PLANE_CAP, 2, FEAT),
            8,
            UPDATE_FLOPS // 8,
            1_500_000,
            [place], pieces[7:], picked, [before, current, chip_gain],
        )
    back = current[:, :ROWS].T.reshape(OWN, CHIPS, CHIP_FEAT).transpose(1, 0, 2)
    back = lax.all_to_all(back, ("z", "x"), split_axis=0, concat_axis=0, tiled=True)
    decoded = back.transpose(1, 0, 2).reshape(OWN, D)
    return (master_new, moment_new, second_new, decoded)


def solution(mesh):
    mesh = jax.sharding.Mesh(mesh.devices.reshape(NY, NZ, NX, NC), ("dp",) + EXPERT)
    placed = (
        P("dp", None),
        P("dp", EXPERT),
        P("dp", EXPERT),
        P("dp", EXPERT),
        P("dp", EXPERT),
        P(),
        P(EXPERT, None),
        P(EXPERT, None),
        P(),
        P(("dp",) + EXPERT, None),
        P(("dp",) + EXPERT, None),
        P(("dp",) + EXPERT, None),
    )
    return jax.shard_map(
        local,
        mesh=mesh,
        in_specs=placed,
        out_specs=(
            P("dp", EXPERT),
            P("dp", EXPERT),
            P("dp", EXPERT),
            P(("dp",) + EXPERT, None),
        ),
        check_vma=False,
    )
```

```python
import jax
import jax.numpy as jnp
from jax import lax
from jax.experimental import pallas as pl
from jax.experimental.pallas import tpu as pltpu
from jax.sharding import PartitionSpec as P

D = 7168
FF = 2048
STEPS = 2
ADAM_STEP = 10
UNITS = 8192
FLIGHT = 4
CAP = 192
OWNERS = 64
NZ, NX, NC, NY = 8, 4, 2, 4
CHIPS = NZ * NX
FEAT = D // OWNERS
CHIP_FEAT = D // CHIPS
CHIP_CAP = NC * CAP
BLOCK = UNITS // NY
OWN = 3
ROWS = OWN * CHIPS
TAIL = 128 - ROWS
ROW_MAIN = 176
HID_MAIN = 288
CHUNKS = D // 128
PLANE_CAP = NX * CHIP_CAP
X_ORDER = (0, 3, 1, 2)
TILE = 512
EXPERT = ("z", "x", "c")
Z_ORDER = (0, 7, 1, 6, 2, 5, 3, 4, 4)
BF = jnp.bfloat16
F32 = jnp.float32


def send(value, axis, size, by):
    return lax.ppermute(value, axis, [(i, (i + by) % size) for i in range(size)])


def together(*values):
    return lax.optimization_barrier(values)


def gather_chips(shard, ties=()):
    four = jnp.stack([shard] + [send(shard, "x", NX, by) for by in (1, 3, 2)])
    tied = []
    if ties:
        four, first = together(four, ties[0])
        tied.append(first)
    pieces, up, down = [four], four, four
    for step in range(3):
        up, down = send(up, "z", NZ, 1), send(down, "z", NZ, -1)
        if step + 1 < len(ties):
            up, down, one = together(up, down, ties[step + 1])
            tied.append(one)
        pieces += [up, down]
    return pieces + [send(up[:2], "z", NZ, 1), send(down[2:], "z", NZ, -1)], tied


def gather_rows(shard, ties=()):
    eight = jnp.stack([shard] + [send(shard, "z", NZ, -d) for d in Z_ORDER[1:8]])
    tied = []
    if ties:
        eight, *tied = together(eight, ties[0])
    left, right = send(eight, "x", NX, 1), send(eight, "x", NX, -1)
    if ties:
        left, right, *rest = together(left, right, *ties[1:])
        tied += rest
    far = [send(left[:4], "x", NX, 1), send(right[4:], "x", NX, -1)]
    return [eight, left, right] + far, tied


COLUMNS = ((0, 0), (3, 0), (1, 0), (2, 0), (2, 4))


def each_row_shard(place, pieces, body):
    for (dx, first), piece in zip(COLUMNS, pieces):
        x = lax.rem(place[1] + dx, NX)
        for j in range(piece.shape[0]):
            body(lax.rem(place[0] + Z_ORDER[first + j], NZ) * NX + x, piece[j])


def pack(full, main, extra=()):
    parts = [full[main:, k : k + TAIL] for k in range(0, ROWS, TAIL)]
    parts += [row[:, k : k + TAIL] for row in extra for k in range(0, ROWS, TAIL)]
    missing = main - sum(part.shape[0] for part in parts)
    if missing:
        parts.append(jnp.zeros((missing, TAIL), full.dtype))
    return jnp.concatenate([full[:main, :ROWS], jnp.concatenate(parts, axis=0)], axis=1)


def unpack(shard, whole, at, size, main):
    rest = size - main
    whole[pl.ds(pl.multiple_of(at, 16), main), :] = shard[:main]
    parts = [shard[k * rest : (k + 1) * rest, ROWS:] for k in range(3)]
    whole[pl.ds(pl.multiple_of(at + main, 16), rest), :] = jnp.concatenate(
        parts + parts[:1], axis=1
    )


def unpack_plane(place, piece, first, plane):
    for j in range(piece.shape[0]):
        x = lax.rem(place[1] + X_ORDER[first + j], NX)
        unpack(piece[j], plane, x * CHIP_CAP, CHIP_CAP, HID_MAIN)


def plane_copies(place, planes, width, sources, held, sems):
    copies = []
    for i, plane in enumerate(planes):
        at = pl.multiple_of(lax.rem(place[0] + Z_ORDER[plane], NZ) * width, 128)
        copies.append([
            pltpu.make_async_copy(source.at[:, pl.ds(at, width)], held.at[i, k], sems.at[i, k])
            for k, source in enumerate(sources)
        ])
    for row in copies:
        for copy in row:
            copy.start()
    return copies


HALF = D // 2


def weight_copies(sources, held, sems):
    return [
        [
            pltpu.make_async_copy(
                source.at[:, pl.ds(half * HALF, HALF)],
                held.at[k, :, pl.ds(half * HALF, HALF)],
                sems.at[half, k],
            )
            for k, source in enumerate(sources)
        ]
        for half in range(2)
    ]


def experts(whole, square, copies, held, slot_weight, core, both):
    total = jnp.zeros((4 * CAP, 128), F32)
    for half in range(2):
        for copy in copies[half]:
            copy.wait()
        for at in range(half * HALF, (half + 1) * HALF, TILE):
            part = held[:, :, at : at + TILE].reshape(4 * CAP, TILE)
            total += jnp.dot(part, whole[at : at + TILE], preferred_element_type=F32)
    totals = [total[k * CAP : (k + 1) * CAP] for k in range(4)]
    return activated(totals, square, slot_weight, core, both)


def activated(totals, square, slot_weight, core, both):
    scale = lax.rsqrt(square * (1.0 / D) + 1e-06)
    for k in range(2):
        first, second = totals[2 * k] * scale, totals[2 * k + 1] * scale
        at = pl.multiple_of((core if k == 0 else 1 - core) * CAP, 8)
        both[pl.ds(at, CAP), :] = first * (1.0 / (1.0 + jnp.exp(-first))) * second
    return both[...] * slot_weight


def first_kernel(place, *refs):
    pieces, weights = refs[:5], refs[5:9]
    slot_expert, gain, out, current, slot_weight, rows, turn, whole, both, held, sems = refs[9:]
    copies = weight_copies(weights, held, sems)
    for copy in copies[0] + copies[1]:
        copy.start()

    def body(chip, shard):
        rows[pl.ds(pl.multiple_of(chip * ROW_MAIN, 8), ROW_MAIN), :] = shard.astype(F32)

    each_row_shard(place, pieces, body)

    def chunk(at):
        parts = [rows[pl.ds(at + step, CHIPS, stride=ROW_MAIN), :] for step in (0, CHUNKS, 2 * CHUNKS)]
        parts.append(jnp.zeros((TAIL, 128), F32))
        return jnp.concatenate(parts, axis=0)

    square = jnp.zeros((128, 128), F32)
    for k in range(CHUNKS):
        values = chunk(k)
        square += values * values
        whole[k * 128 : (k + 1) * 128, :] = (values * gain[k : k + 1, :]).T.astype(BF)
    square = jnp.sum(square.T, axis=0, keepdims=True)
    picks = [rows[pl.ds(OWN * CHUNKS + t, CHIPS, stride=ROW_MAIN), :] for t in range(OWN)]
    weight = jnp.concatenate(picks + [jnp.zeros((TAIL, 128), F32)], axis=0).T
    expert = slot_expert[...]
    slots = jnp.zeros((CHIP_CAP, 128), F32)
    for k in range(FLIGHT):
        slots += jnp.where(expert == k, weight[k : k + 1], 0.0)
    slot_weight[...] = slots
    at = (place[0] * NX + place[1]) * CHIP_FEAT
    base = jnp.minimum(at // 128, CHUNKS - 3)
    for k in range(3):
        turn[k * 128 : (k + 1) * 128, :] = chunk(base + k).T
    current[...] = turn[pl.ds(pl.multiple_of(at - base * 128, 8), CHIP_FEAT), :].astype(BF)
    hidden = experts(whole, square, copies, held, slots, place[2], both)
    out[...] = pack(hidden, HID_MAIN).astype(BF)


def gate_up_kernel(place, *refs):
    pieces, weights = refs[:5], refs[5:9]
    slot_weight, out, extra, whole, both, held, sems = refs[9:]
    copies = weight_copies(weights, held, sems)
    for copy in copies[0] + copies[1]:
        copy.start()
    extra[...] = jnp.zeros(extra.shape, F32)

    def body(chip, shard):
        unpack(shard, whole, chip * CHIP_FEAT, CHIP_FEAT, ROW_MAIN)
        extra[...] += shard[3 * (CHIP_FEAT - ROW_MAIN) :][:16].astype(F32)

    each_row_shard(place, pieces, body)
    sums = extra[0:3, ROWS:] + extra[3:6, ROWS:]
    square = jnp.concatenate([sums[0:1], sums[1:2], sums[2:3], sums[0:1]], axis=1)
    hidden = experts(whole, square, copies, held, slot_weight[...], place[2], both)
    out[...] = pack(hidden, HID_MAIN).astype(BF)


def whole_update_kernel(place, *refs):
    pieces, picked = refs[:9], refs[9:11]
    current, gain, out, packed, whole, both, held, sems = refs[11:]
    copies = [pltpu.make_async_copy(picked[k], held.at[k], sems.at[k]) for k in range(2)]
    for copy in copies:
        copy.start()
    for i, piece in enumerate(pieces):
        base = lax.rem(place[0] + Z_ORDER[i], NZ) * PLANE_CAP
        for j in range(piece.shape[0]):
            x = lax.rem(place[1] + X_ORDER[j + (2 if i == 8 else 0)], NX)
            unpack(piece[j], whole, base + x * CHIP_CAP, CHIP_CAP, HID_MAIN)
    for k, copy in enumerate(copies):
        copy.wait()
        total = jnp.zeros((FEAT, 128), F32)
        for at in range(0, CHIPS * CHIP_CAP, TILE):
            total += jnp.dot(
                held[k, :, at : at + TILE], whole[at : at + TILE], preferred_element_type=F32
            )
        at = pl.multiple_of((place[2] if k == 0 else 1 - place[2]) * FEAT, 8)
        both[pl.ds(at, FEAT), :] = total
    fresh = (current[...].astype(F32) + both[...]).astype(BF)
    out[...] = fresh
    fresh = fresh.astype(F32)
    square = jnp.sum(fresh * fresh, axis=0, keepdims=True)
    high = square.astype(BF).astype(F32)
    packed[...] = pack(fresh * gain[...], ROW_MAIN, (high, square - high)).astype(BF)


def update_kernel(place, *refs):
    pieces, picked = refs[:7], refs[7:9]
    out, planes, held, sems = refs[9:]
    copies = plane_copies(place, range(7), PLANE_CAP, picked, held, sems)
    totals = [jnp.zeros((FEAT, 128), F32) for _ in range(2)]
    for i in range(7):
        unpack_plane(place, pieces[i], 0, planes.at[i])
        for k in range(2):
            copies[i][k].wait()
            totals[k] += jnp.dot(held[i, k], planes[i], preferred_element_type=F32)
    for k in range(2):
        out[k] = totals[k]


def update_last_kernel(place, *refs):
    pieces, picked = refs[:2], refs[2:4]
    before, current, gain, out, packed, both, plane, held, sems = refs[4:]
    copies = plane_copies(place, (7,), PLANE_CAP, picked, held, sems)
    for i in range(2):
        unpack_plane(place, pieces[i], 2 * i, plane)
    for k in range(2):
        copies[0][k].wait()
        total = before[k] + jnp.dot(held[0, k], plane[...], preferred_element_type=F32)
        at = pl.multiple_of((place[2] if k == 0 else 1 - place[2]) * FEAT, 8)
        both[pl.ds(at, FEAT), :] = total
    fresh = (current[...].astype(F32) + both[...]).astype(BF)
    out[...] = fresh
    fresh = fresh.astype(F32)
    square = jnp.sum(fresh * fresh, axis=0, keepdims=True)
    high = square.astype(BF).astype(F32)
    packed[...] = pack(fresh * gain[...], ROW_MAIN, (high, square - high)).astype(BF)


def pick_kernel(replica, slot_units, b0, b1, b2, b3, out, slab):
    for by, block in zip((0, 1, 3, 2), (b0, b1, b2, b3)):
        at = lax.rem(replica[0] + NY - by, NY) * BLOCK
        slab[:, pl.ds(pl.multiple_of(at, BLOCK), BLOCK)] = block[...]
    slab[:, UNITS:] = jnp.zeros((FEAT, 256), BF)
    lane = lax.broadcasted_iota(jnp.int32, (FEAT, 128), 1)

    def window(owner, lead):
        start = slot_units[owner * CAP]
        base = start // 128
        off = start - base * 128
        tiles = []
        for k in range(3):
            tile = slab[:, pl.ds(pl.multiple_of((base + k) * 128, 128), 128)].astype(F32)
            tiles.append(pltpu.roll(tile, lax.rem(128 - off + lead, 128), 1))
        return off, tiles

    def pair(p, carry):
        off, (r0, r1, r2) = window(2 * p, 0)
        out0 = jnp.where(lane < 128 - off, r0, r1)
        out1 = jnp.where(lane < 128 - off, r1, r2)
        off, (r0, r1, r2) = window(2 * p + 1, 64)
        late = jnp.where(lane < 192 - off, r0, r1)
        out2 = jnp.where(lane < 64 - off, r0, jnp.where(lane < 192 - off, r1, r2))
        out1 = jnp.where(lane < 64, out1, late)
        both = jnp.concatenate([out0, out1, out2], axis=1).astype(BF)
        out[:, pl.ds(pl.multiple_of(p * 384, 384), 384)] = both
        return carry

    lax.fori_loop(0, OWNERS // 2, pair, 0)


SMEM = pl.BlockSpec(memory_space=pltpu.SMEM)
VMEM = pl.BlockSpec(memory_space=pltpu.VMEM)
FAR = pl.BlockSpec(memory_space=pl.ANY)


def shape(*dims, dtype=BF):
    return jax.ShapeDtypeStruct(dims, dtype)


def call(kernel, outs, scratch, vmem, flops, moved_bytes, scalars, near, far=(), last=()):
    return pl.pallas_call(
        kernel,
        out_shape=outs,
        in_specs=[SMEM] * len(scalars) + [VMEM] * len(near) + [FAR] * len(far) + [VMEM] * len(last),
        out_specs=jax.tree.map(lambda _: VMEM, outs),
        scratch_shapes=scratch,
        compiler_params=pltpu.CompilerParams(vmem_limit_bytes=vmem * 1024 * 1024),
        cost_estimate=pl.CostEstimate(flops=flops, bytes_accessed=moved_bytes, transcendentals=0),
    )(*scalars, *near, *far, *last)


GATE_SCRATCH = [
    pltpu.VMEM((D, 128), BF),
    pltpu.VMEM((CHIP_CAP, 128), F32),
    pltpu.VMEM((4, CAP, D), BF),
    pltpu.SemaphoreType.DMA((2, 4)),
]
UPDATE_SCRATCH = [
    pltpu.VMEM((CHIPS * CHIP_CAP, 128), BF),
    pltpu.VMEM((CHIP_FEAT, 128), F32),
    pltpu.VMEM((2, FEAT, CHIPS * CHIP_CAP), BF),
    pltpu.SemaphoreType.DMA((2,)),
]


def plane_scratch(planes, width, sources, rows):
    lead = (planes,) if planes > 1 else ()
    return [
        pltpu.VMEM(lead + (width, 128), BF),
        pltpu.VMEM((planes, sources, rows, width), BF),
        pltpu.SemaphoreType.DMA((planes, sources)),
    ]


GATE_FLOPS = 2 * 2 * CHIP_CAP * D * 128
UPDATE_FLOPS = 2 * CHIP_FEAT * CHIPS * CHIP_CAP * 128


def local(
    learner_hidden,
    learner_cot,
    master,
    moment_one,
    moment_two,
    slot_units,
    gate_slots,
    up_slots,
    norm_gain,
    tokens,
    routes,
    gate_weights,
):
    replica = lax.axis_index("dp")
    z, x, c = (lax.axis_index(axis) for axis in EXPERT)
    place = jnp.stack([z, x, c]).astype(jnp.int32)
    chip = z * NX + x

    expert_ids = jnp.arange(FLIGHT, dtype=jnp.int32)
    picks = (routes[:, :, None] == expert_ids[None, None, :]).astype(F32)
    weight = jnp.sum(gate_weights.astype(F32)[:, :, None] * picks, axis=1).astype(BF)
    below = jnp.pad(weight, ((0, ROW_MAIN - OWN * CHUNKS - OWN), (0, 128 - FLIGHT)))
    packed = jnp.concatenate([tokens.reshape(OWN * CHUNKS, 128), below], axis=0)

    grad = lax.dot_general(
        learner_hidden, learner_cot, (((0,), (0,)), ((), ())), preferred_element_type=F32
    )
    grad = grad.astype(BF)

    def block_for(by):
        return lax.dynamic_slice_in_dim(grad, (replica + by) % NY * BLOCK, BLOCK, 0)

    outgoing = [block_for(by) for by in (1, 3, 2)]
    packed, *outgoing = together(packed, *outgoing)
    arriving = [send(block, "dp", NY, by) for block, by in zip(outgoing, (1, 3, 2))]
    pieces, arriving = gather_rows(packed, arriving)
    grad = sum(part.astype(F32) for part in [block_for(0), *arriving])
    moment_new = 0.9 * moment_one + 0.1 * grad
    second_new = 0.95 * moment_two + 0.05 * grad * grad
    corr_first = 1.0 - 0.9**ADAM_STEP
    corr_second = 1.0 - 0.95**ADAM_STEP
    master_new = master - 0.005 * (
        moment_new / corr_first / (jnp.sqrt(second_new / corr_second) + 1e-08) + 0.1 * master
    )
    slab = master_new.astype(BF).T

    weights = [gate_slots, up_slots] + [send(own, "c", NC, 1) for own in (gate_slots, up_slots)]
    gain = norm_gain.astype(F32)
    chip_gain = lax.dynamic_slice_in_dim(gain, chip * CHIP_FEAT, CHIP_FEAT)[:, None]
    chip_slots = lax.dynamic_slice_in_dim(slot_units, chip * CHIP_CAP, CHIP_CAP)
    slot_expert = jnp.where(chip_slots < UNITS, chip_slots // FF, -1)[:, None]
    hidden, current, slot_weight = call(
        first_kernel,
        (shape(HID_MAIN, 128), shape(CHIP_FEAT, 128), shape(CHIP_CAP, 128, dtype=F32)),
        [pltpu.VMEM((CHIPS * ROW_MAIN, 128), F32), pltpu.VMEM((384, 128), F32)] + GATE_SCRATCH,
        28,
        GATE_FLOPS,
        13_000_000,
        [place], pieces, weights, [slot_expert, gain.reshape(CHUNKS, 128)],
    )
    hidden, slab = together(hidden, slab)
    blocks = [send(slab, "dp", NY, by) for by in (1, 3, 2)]
    for step_index in range(STEPS):
        if step_index:
            pieces, _ = gather_rows(packed)
            hidden = call(
                gate_up_kernel,
                shape(HID_MAIN, 128),
                [pltpu.VMEM((16, 128), F32)] + GATE_SCRATCH,
                24,
                GATE_FLOPS,
                13_000_000,
                [place], pieces, weights, [slot_weight],
            )
        pieces, tied = gather_chips(hidden, () if step_index else blocks)
        if step_index == 0:
            own_picked = call(
                pick_kernel,
                shape(FEAT, OWNERS * CAP),
                [pltpu.VMEM((FEAT, UNITS + 256), BF)],
                14,
                0,
                5_000_000,
                [lax.axis_index("dp").astype(jnp.int32)[None], slot_units], [slab, *tied],
            )
            picked = [own_picked, send(own_picked, "c", NC, 1)]
            current, packed = call(
                whole_update_kernel,
                (shape(CHIP_FEAT, 128), shape(ROW_MAIN, 128)),
                UPDATE_SCRATCH,
                18,
                UPDATE_FLOPS,
                8_000_000,
                [place], pieces, picked, [current, chip_gain],
            )
            continue
        before = call(
            update_kernel,
            shape(2, FEAT, 128, dtype=F32),
            plane_scratch(7, PLANE_CAP, 2, FEAT),
            18,
            UPDATE_FLOPS * 7 // 8,
            7_000_000,
            [place], pieces[:7], picked,
        )
        current, packed = call(
            update_last_kernel,
            (shape(CHIP_FEAT, 128), shape(ROW_MAIN, 128)),
            [pltpu.VMEM((CHIP_FEAT, 128), F32)] + plane_scratch(1, PLANE_CAP, 2, FEAT),
            8,
            UPDATE_FLOPS // 8,
            1_500_000,
            [place], pieces[7:], picked, [before, current, chip_gain],
        )
    back = current[:, :ROWS].T.reshape(OWN, CHIPS, CHIP_FEAT).transpose(1, 0, 2)
    back = lax.all_to_all(back, ("z", "x"), split_axis=0, concat_axis=0, tiled=True)
    decoded = back.transpose(1, 0, 2).reshape(OWN, D)
    return (master_new, moment_new, second_new, decoded)


def solution(mesh):
    mesh = jax.sharding.Mesh(mesh.devices.reshape(NY, NZ, NX, NC), ("dp",) + EXPERT)
    placed = (
        P("dp", None),
        P("dp", EXPERT),
        P("dp", EXPERT),
        P("dp", EXPERT),
        P("dp", EXPERT),
        P(),
        P(EXPERT, None),
        P(EXPERT, None),
        P(),
        P(("dp",) + EXPERT, None),
        P(("dp",) + EXPERT, None),
        P(("dp",) + EXPERT, None),
    )
    return jax.shard_map(
        local,
        mesh=mesh,
        in_specs=placed,
        out_specs=(
            P("dp", EXPERT),
            P("dp", EXPERT),
            P("dp", EXPERT),
            P(("dp",) + EXPERT, None),
        ),
        check_vma=False,
    )
```

```python
import functools

import jax
import jax.numpy as jnp
from jax import lax
from jax.experimental import pallas as pl
from jax.experimental.pallas import tpu as pltpu
from jax.sharding import PartitionSpec as P

D = 7168
FF = 2048
STEPS = 2
ADAM_STEP = 10
UNITS = 8192
FLIGHT = 4
CAP = 192
OWNERS = 64
NZ, NX, NC, NY = 8, 4, 2, 4
CHIPS = NZ * NX
FEAT = D // OWNERS
CHIP_FEAT = D // CHIPS
CHIP_CAP = NC * CAP
BLOCK = UNITS // NY
OWN = 3
ROWS = OWN * CHIPS
TAIL = 128 - ROWS
ROW_MAIN = 176
HID_MAIN = 288
CHUNKS = D // 128
PLANE_FEAT = NX * CHIP_FEAT
PLANE_CAP = NX * CHIP_CAP
X_ORDER = (0, 3, 1, 2)
TILE = 512
EXPERT = ("z", "x", "c")
Z_ORDER = (0, 7, 1, 6, 2, 5, 3, 4, 4)
BF = jnp.bfloat16
F32 = jnp.float32


def send(value, axis, size, by):
    return lax.ppermute(value, axis, [(i, (i + by) % size) for i in range(size)])


def together(*values):
    return lax.optimization_barrier(values)


def gather_chips(shard, ties=()):
    four = jnp.stack([shard] + [send(shard, "x", NX, by) for by in (1, 3, 2)])
    tied = []
    if ties:
        four, first = together(four, ties[0])
        tied.append(first)
    pieces, up, down = [four], four, four
    for step in range(3):
        up, down = send(up, "z", NZ, 1), send(down, "z", NZ, -1)
        if step + 1 < len(ties):
            down, one = together(down, ties[step + 1])
            tied.append(one)
        pieces += [up, down]
    return pieces + [send(up[:2], "z", NZ, 1), send(down[2:], "z", NZ, -1)], tied


def each_shard(place, pieces, body):
    for i, piece in enumerate(pieces):
        plane = lax.rem(place[0] + Z_ORDER[i], NZ) * NX
        for j in range(piece.shape[0]):
            x = lax.rem(place[1] + X_ORDER[j + (2 if i == 8 else 0)], NX)
            body(plane + x, piece[j])


def pack(full, main, extra=()):
    parts = [full[main:, k : k + TAIL] for k in range(0, ROWS, TAIL)]
    parts += [row[:, k : k + TAIL] for row in extra for k in range(0, ROWS, TAIL)]
    missing = main - sum(part.shape[0] for part in parts)
    if missing:
        parts.append(jnp.zeros((missing, TAIL), full.dtype))
    return jnp.concatenate([full[:main, :ROWS], jnp.concatenate(parts, axis=0)], axis=1)


def unpack(place, piece, first, plane, size, main, extra=None):
    rest = size - main
    for j in range(piece.shape[0]):
        shard = piece[j]
        at = pl.multiple_of(lax.rem(place[1] + X_ORDER[first + j], NX) * size, 16)
        plane[pl.ds(at, main), :] = shard[:main]
        parts = [shard[k * rest : (k + 1) * rest, ROWS:] for k in range(3)]
        plane[pl.ds(pl.multiple_of(at + main, 16), rest), :] = jnp.concatenate(
            parts + parts[:1], axis=1
        )
        if extra is not None:
            extra[...] += shard[3 * rest : 3 * rest + 16].astype(F32)


def plane_copies(place, planes, width, sources, held, sems):
    copies = []
    for i, plane in enumerate(planes):
        at = pl.multiple_of(lax.rem(place[0] + Z_ORDER[plane], NZ) * width, 128)
        copies.append([
            pltpu.make_async_copy(source.at[:, pl.ds(at, width)], held.at[i, k], sems.at[i, k])
            for k, source in enumerate(sources)
        ])
    for row in copies:
        for copy in row:
            copy.start()
    return copies


HALF = D // 2


def weight_copies(sources, held, sems):
    return [
        [
            pltpu.make_async_copy(
                source.at[:, pl.ds(half * HALF, HALF)],
                held.at[k, :, pl.ds(half * HALF, HALF)],
                sems.at[half, k],
            )
            for k, source in enumerate(sources)
        ]
        for half in range(2)
    ]


def experts(whole, square, copies, held, slot_weight, core, both):
    totals = [jnp.zeros((CAP, 128), F32) for _ in range(4)]
    for half in range(2):
        for copy in copies[half]:
            copy.wait()
        for at in range(half * HALF, (half + 1) * HALF, TILE):
            part = whole[at : at + TILE]
            for k in range(4):
                totals[k] += jnp.dot(held[k, :, at : at + TILE], part, preferred_element_type=F32)
    return activated(totals, square, slot_weight, core, both)


def activated(totals, square, slot_weight, core, both):
    scale = lax.rsqrt(square * (1.0 / D) + 1e-06)
    for k in range(2):
        first, second = totals[2 * k] * scale, totals[2 * k + 1] * scale
        at = pl.multiple_of((core if k == 0 else 1 - core) * CAP, 8)
        both[pl.ds(at, CAP), :] = first * (1.0 / (1.0 + jnp.exp(-first))) * second
    return both[...] * slot_weight


def first_kernel(place, *refs):
    pieces, weights = refs[:9], refs[9:13]
    slot_expert, gain, out, current, slot_weight, rows, turn, whole, both, held, sems = refs[13:]
    copies = weight_copies(weights, held, sems)
    for copy in copies[0] + copies[1]:
        copy.start()

    def body(chip, shard):
        rows[pl.ds(pl.multiple_of(chip * ROW_MAIN, 8), ROW_MAIN), :] = shard.astype(F32)

    each_shard(place, pieces, body)

    def chunk(at):
        parts = [rows[pl.ds(at + step, CHIPS, stride=ROW_MAIN), :] for step in (0, CHUNKS, 2 * CHUNKS)]
        parts.append(jnp.zeros((TAIL, 128), F32))
        return jnp.concatenate(parts, axis=0)

    square = jnp.zeros((128, 128), F32)
    for k in range(CHUNKS):
        values = chunk(k)
        square += values * values
        whole[k * 128 : (k + 1) * 128, :] = (values * gain[k : k + 1, :]).T.astype(BF)
    square = jnp.sum(square.T, axis=0, keepdims=True)
    picks = [rows[pl.ds(OWN * CHUNKS + t, CHIPS, stride=ROW_MAIN), :] for t in range(OWN)]
    weight = jnp.concatenate(picks + [jnp.zeros((TAIL, 128), F32)], axis=0).T
    expert = slot_expert[...]
    slots = jnp.zeros((CHIP_CAP, 128), F32)
    for k in range(FLIGHT):
        slots += jnp.where(expert == k, weight[k : k + 1], 0.0)
    slot_weight[...] = slots
    at = (place[0] * NX + place[1]) * CHIP_FEAT
    base = jnp.minimum(at // 128, CHUNKS - 3)
    for k in range(3):
        turn[k * 128 : (k + 1) * 128, :] = chunk(base + k).T
    current[...] = turn[pl.ds(pl.multiple_of(at - base * 128, 8), CHIP_FEAT), :].astype(BF)
    hidden = experts(whole, square, copies, held, slots, place[2], both)
    out[...] = pack(hidden, HID_MAIN).astype(BF)


def gate_up_kernel(first, count, place, *refs):
    pieces, weights = refs[:count], refs[count : count + 4]
    refs = refs[count + 4 :]
    copies = plane_copies(place, range(first, first + count), PLANE_FEAT, weights, *refs[-2:])
    if first:
        before, extra_before, out, extra, planes, held, _ = refs
        extra[...] = extra_before[...]
        totals = [before[k] for k in range(4)]
    else:
        out, extra, planes, held, _ = refs
        extra[...] = jnp.zeros(extra.shape, F32)
        totals = [jnp.zeros((CAP, 128), F32) for _ in range(4)]
    for i in range(count):
        unpack(place, pieces[i], 0, planes.at[i], CHIP_FEAT, ROW_MAIN, extra)
        for k in range(4):
            copies[i][k].wait()
            totals[k] += jnp.dot(held[i, k], planes[i], preferred_element_type=F32)
    for k in range(4):
        out[k] = totals[k]


def gate_up_last_kernel(place, *refs):
    pieces, weights = refs[:2], refs[2:6]
    before, extra_before, slot_weight, out, extra, both, plane, held, sems = refs[6:]
    copies = plane_copies(place, (7,), PLANE_FEAT, weights, held, sems)
    extra[...] = extra_before[...]
    for i in range(2):
        unpack(place, pieces[i], 2 * i, plane, CHIP_FEAT, ROW_MAIN, extra)
    totals = []
    for k in range(4):
        copies[0][k].wait()
        totals.append(before[k] + jnp.dot(held[0, k], plane[...], preferred_element_type=F32))
    sums = extra[0:3, ROWS:] + extra[3:6, ROWS:]
    square = jnp.concatenate([sums[0:1], sums[1:2], sums[2:3], sums[0:1]], axis=1)
    hidden = activated(totals, square, slot_weight[...], place[2], both)
    out[...] = pack(hidden, HID_MAIN).astype(BF)


def whole_update_kernel(place, *refs):
    pieces, picked = refs[:9], refs[9:11]
    current, gain, out, packed, whole, both, held, sems = refs[11:]
    copies = [pltpu.make_async_copy(picked[k], held.at[k], sems.at[k]) for k in range(2)]
    for copy in copies:
        copy.start()
    for i, piece in enumerate(pieces):
        base = pl.multiple_of(lax.rem(place[0] + Z_ORDER[i], NZ) * PLANE_CAP, 128)
        plane = whole.at[pl.ds(base, PLANE_CAP)]
        unpack(place, piece, 2 if i == 8 else 0, plane, CHIP_CAP, HID_MAIN)
    for k, copy in enumerate(copies):
        copy.wait()
        total = jnp.zeros((FEAT, 128), F32)
        for at in range(0, CHIPS * CHIP_CAP, TILE):
            total += jnp.dot(
                held[k, :, at : at + TILE], whole[at : at + TILE], preferred_element_type=F32
            )
        at = pl.multiple_of((place[2] if k == 0 else 1 - place[2]) * FEAT, 8)
        both[pl.ds(at, FEAT), :] = total
    fresh = (current[...].astype(F32) + both[...]).astype(BF)
    out[...] = fresh
    fresh = fresh.astype(F32)
    square = jnp.sum(fresh * fresh, axis=0, keepdims=True)
    high = square.astype(BF).astype(F32)
    packed[...] = pack(fresh * gain[...], ROW_MAIN, (high, square - high)).astype(BF)


def update_kernel(place, *refs):
    pieces, picked = refs[:7], refs[7:9]
    out, planes, held, sems = refs[9:]
    copies = plane_copies(place, range(7), PLANE_CAP, picked, held, sems)
    totals = [jnp.zeros((FEAT, 128), F32) for _ in range(2)]
    for i in range(7):
        unpack(place, pieces[i], 0, planes.at[i], CHIP_CAP, HID_MAIN)
        for k in range(2):
            copies[i][k].wait()
            totals[k] += jnp.dot(held[i, k], planes[i], preferred_element_type=F32)
    for k in range(2):
        out[k] = totals[k]


def update_last_kernel(place, *refs):
    pieces, picked = refs[:2], refs[2:4]
    before, current, gain, out, packed, both, plane, held, sems = refs[4:]
    copies = plane_copies(place, (7,), PLANE_CAP, picked, held, sems)
    for i in range(2):
        unpack(place, pieces[i], 2 * i, plane, CHIP_CAP, HID_MAIN)
    for k in range(2):
        copies[0][k].wait()
        total = before[k] + jnp.dot(held[0, k], plane[...], preferred_element_type=F32)
        at = pl.multiple_of((place[2] if k == 0 else 1 - place[2]) * FEAT, 8)
        both[pl.ds(at, FEAT), :] = total
    fresh = (current[...].astype(F32) + both[...]).astype(BF)
    out[...] = fresh
    fresh = fresh.astype(F32)
    square = jnp.sum(fresh * fresh, axis=0, keepdims=True)
    high = square.astype(BF).astype(F32)
    packed[...] = pack(fresh * gain[...], ROW_MAIN, (high, square - high)).astype(BF)


def pick_kernel(replica, slot_units, b0, b1, b2, b3, out, slab):
    for by, block in zip((0, 1, 3, 2), (b0, b1, b2, b3)):
        at = lax.rem(replica[0] + NY - by, NY) * BLOCK
        slab[:, pl.ds(pl.multiple_of(at, BLOCK), BLOCK)] = block[...]
    slab[:, UNITS:] = jnp.zeros((FEAT, 256), BF)
    lane = lax.broadcasted_iota(jnp.int32, (FEAT, 128), 1)

    def window(owner, lead):
        start = slot_units[owner * CAP]
        base = start // 128
        off = start - base * 128
        tiles = []
        for k in range(3):
            tile = slab[:, pl.ds(pl.multiple_of((base + k) * 128, 128), 128)].astype(F32)
            tiles.append(pltpu.roll(tile, lax.rem(128 - off + lead, 128), 1))
        return off, tiles

    def pair(p, carry):
        off, (r0, r1, r2) = window(2 * p, 0)
        out0 = jnp.where(lane < 128 - off, r0, r1)
        out1 = jnp.where(lane < 128 - off, r1, r2)
        off, (r0, r1, r2) = window(2 * p + 1, 64)
        late = jnp.where(lane < 192 - off, r0, r1)
        out2 = jnp.where(lane < 64 - off, r0, jnp.where(lane < 192 - off, r1, r2))
        out1 = jnp.where(lane < 64, out1, late)
        both = jnp.concatenate([out0, out1, out2], axis=1).astype(BF)
        out[:, pl.ds(pl.multiple_of(p * 384, 384), 384)] = both
        return carry

    lax.fori_loop(0, OWNERS // 2, pair, 0)


SMEM = pl.BlockSpec(memory_space=pltpu.SMEM)
VMEM = pl.BlockSpec(memory_space=pltpu.VMEM)
FAR = pl.BlockSpec(memory_space=pl.ANY)


def shape(*dims, dtype=BF):
    return jax.ShapeDtypeStruct(dims, dtype)


def call(kernel, outs, scratch, vmem, flops, moved_bytes, scalars, near, far=(), last=()):
    return pl.pallas_call(
        kernel,
        out_shape=outs,
        in_specs=[SMEM] * len(scalars) + [VMEM] * len(near) + [FAR] * len(far) + [VMEM] * len(last),
        out_specs=jax.tree.map(lambda _: VMEM, outs),
        scratch_shapes=scratch,
        compiler_params=pltpu.CompilerParams(vmem_limit_bytes=vmem * 1024 * 1024),
        cost_estimate=pl.CostEstimate(flops=flops, bytes_accessed=moved_bytes, transcendentals=0),
    )(*scalars, *near, *far, *last)


GATE_SCRATCH = [
    pltpu.VMEM((D, 128), BF),
    pltpu.VMEM((CHIP_CAP, 128), F32),
    pltpu.VMEM((4, CAP, D), BF),
    pltpu.SemaphoreType.DMA((2, 4)),
]


UPDATE_SCRATCH = [
    pltpu.VMEM((CHIPS * CHIP_CAP, 128), BF),
    pltpu.VMEM((CHIP_FEAT, 128), F32),
    pltpu.VMEM((2, FEAT, CHIPS * CHIP_CAP), BF),
    pltpu.SemaphoreType.DMA((2,)),
]


def plane_scratch(planes, width, sources, rows):
    lead = (planes,) if planes > 1 else ()
    return [
        pltpu.VMEM(lead + (width, 128), BF),
        pltpu.VMEM((planes, sources, rows, width), BF),
        pltpu.SemaphoreType.DMA((planes, sources)),
    ]


GATE_FLOPS = 2 * 2 * CHIP_CAP * D * 128
UPDATE_FLOPS = 2 * CHIP_FEAT * CHIPS * CHIP_CAP * 128


def local(
    learner_hidden,
    learner_cot,
    master,
    moment_one,
    moment_two,
    slot_units,
    gate_slots,
    up_slots,
    norm_gain,
    tokens,
    routes,
    gate_weights,
):
    replica = lax.axis_index("dp")
    z, x, c = (lax.axis_index(axis) for axis in EXPERT)
    place = jnp.stack([z, x, c]).astype(jnp.int32)
    chip = z * NX + x

    expert_ids = jnp.arange(FLIGHT, dtype=jnp.int32)
    picks = (routes[:, :, None] == expert_ids[None, None, :]).astype(F32)
    weight = jnp.sum(gate_weights.astype(F32)[:, :, None] * picks, axis=1).astype(BF)
    below = jnp.pad(weight, ((0, ROW_MAIN - OWN * CHUNKS - OWN), (0, 128 - FLIGHT)))
    packed = jnp.concatenate([tokens.reshape(OWN * CHUNKS, 128), below], axis=0)

    grad = lax.dot_general(
        learner_hidden, learner_cot, (((0,), (0,)), ((), ())), preferred_element_type=F32
    )
    grad = grad.astype(BF)

    def block_for(by):
        return lax.dynamic_slice_in_dim(grad, (replica + by) % NY * BLOCK, BLOCK, 0)

    outgoing = [block_for(by) for by in (1, 3, 2)]
    packed, *outgoing = together(packed, *outgoing)
    arriving = [send(block, "dp", NY, by) for block, by in zip(outgoing, (1, 3, 2))]
    pieces, arriving = gather_chips(packed, arriving)
    grad = sum(part.astype(F32) for part in [block_for(0), *arriving])
    moment_new = 0.9 * moment_one + 0.1 * grad
    second_new = 0.95 * moment_two + 0.05 * grad * grad
    corr_first = 1.0 - 0.9**ADAM_STEP
    corr_second = 1.0 - 0.95**ADAM_STEP
    master_new = master - 0.005 * (
        moment_new / corr_first / (jnp.sqrt(second_new / corr_second) + 1e-08) + 0.1 * master
    )
    slab = master_new.astype(BF).T

    weights = [gate_slots, up_slots] + [send(own, "c", NC, 1) for own in (gate_slots, up_slots)]
    gain = norm_gain.astype(F32)
    chip_gain = lax.dynamic_slice_in_dim(gain, chip * CHIP_FEAT, CHIP_FEAT)[:, None]
    chip_slots = lax.dynamic_slice_in_dim(slot_units, chip * CHIP_CAP, CHIP_CAP)
    slot_expert = jnp.where(chip_slots < UNITS, chip_slots // FF, -1)[:, None]
    hidden, current, slot_weight = call(
        first_kernel,
        (shape(HID_MAIN, 128), shape(CHIP_FEAT, 128), shape(CHIP_CAP, 128, dtype=F32)),
        [pltpu.VMEM((CHIPS * ROW_MAIN, 128), F32), pltpu.VMEM((384, 128), F32)] + GATE_SCRATCH,
        28,
        GATE_FLOPS,
        13_000_000,
        [place], pieces, weights, [slot_expert, gain.reshape(CHUNKS, 128)],
    )
    hidden, slab = together(hidden, slab)
    blocks = [send(slab, "dp", NY, by) for by in (1, 3, 2)]
    for step_index in range(STEPS):
        if step_index:
            pieces, _ = gather_chips(packed)
            sums = []
            for first, count in ((0, 3), (3, 4)):
                sums = call(
                    functools.partial(gate_up_kernel, first, count),
                    (shape(4, CAP, 128, dtype=F32), shape(16, 128, dtype=F32)),
                    plane_scratch(count, PLANE_FEAT, 4, CAP),
                    24,
                    GATE_FLOPS * count // 8,
                    1_500_000 * count,
                    [place], pieces[first : first + count], weights, sums,
                )
            before, extra = sums
            hidden = call(
                gate_up_last_kernel,
                shape(HID_MAIN, 128),
                [pltpu.VMEM((16, 128), F32), pltpu.VMEM((CHIP_CAP, 128), F32)]
                + plane_scratch(1, PLANE_FEAT, 4, CAP),
                8,
                GATE_FLOPS // 8,
                2_000_000,
                [place], pieces[7:], weights, [before, extra, slot_weight],
            )
        pieces, tied = gather_chips(hidden, () if step_index else blocks)
        if step_index == 0:
            own_picked = call(
                pick_kernel,
                shape(FEAT, OWNERS * CAP),
                [pltpu.VMEM((FEAT, UNITS + 256), BF)],
                14,
                0,
                5_000_000,
                [lax.axis_index("dp").astype(jnp.int32)[None], slot_units], [slab, *tied],
            )
            picked = [own_picked, send(own_picked, "c", NC, 1)]
            current, packed = call(
                whole_update_kernel,
                (shape(CHIP_FEAT, 128), shape(ROW_MAIN, 128)),
                UPDATE_SCRATCH,
                18,
                UPDATE_FLOPS,
                8_000_000,
                [place], pieces, picked, [current, chip_gain],
            )
            continue
        before = call(
            update_kernel,
            shape(2, FEAT, 128, dtype=F32),
            plane_scratch(7, PLANE_CAP, 2, FEAT),
            18,
            UPDATE_FLOPS * 7 // 8,
            7_000_000,
            [place], pieces[:7], picked,
        )
        current, packed = call(
            update_last_kernel,
            (shape(CHIP_FEAT, 128), shape(ROW_MAIN, 128)),
            [pltpu.VMEM((CHIP_FEAT, 128), F32)] + plane_scratch(1, PLANE_CAP, 2, FEAT),
            8,
            UPDATE_FLOPS // 8,
            1_500_000,
            [place], pieces[7:], picked, [before, current, chip_gain],
        )
    back = current[:, :ROWS].T.reshape(OWN, CHIPS, CHIP_FEAT).transpose(1, 0, 2)
    back = lax.all_to_all(back, ("z", "x"), split_axis=0, concat_axis=0, tiled=True)
    decoded = back.transpose(1, 0, 2).reshape(OWN, D)
    return (master_new, moment_new, second_new, decoded)


def solution(mesh):
    mesh = jax.sharding.Mesh(mesh.devices.reshape(NY, NZ, NX, NC), ("dp",) + EXPERT)
    placed = (
        P("dp", None),
        P("dp", EXPERT),
        P("dp", EXPERT),
        P("dp", EXPERT),
        P("dp", EXPERT),
        P(),
        P(EXPERT, None),
        P(EXPERT, None),
        P(),
        P(("dp",) + EXPERT, None),
        P(("dp",) + EXPERT, None),
        P(("dp",) + EXPERT, None),
    )
    return jax.shard_map(
        local,
        mesh=mesh,
        in_specs=placed,
        out_specs=(
            P("dp", EXPERT),
            P("dp", EXPERT),
            P("dp", EXPERT),
            P(("dp",) + EXPERT, None),
        ),
        check_vma=False,
    )
```

```python
import jax
import jax.numpy as jnp
from jax import lax
from jax.experimental import pallas as pl
from jax.experimental.pallas import tpu as pltpu
from jax.sharding import PartitionSpec as P

D = 7168
FF = 2048
STEPS = 2
ADAM_STEP = 10
UNITS = 8192
FLIGHT = 4
CAP = 192
OWNERS = 64
NZ, NX, NC, NY = 8, 4, 2, 4
CHIPS = NZ * NX
FEAT = D // OWNERS
CHIP_FEAT = D // CHIPS
CHIP_CAP = NC * CAP
BLOCK = UNITS // NY
OWN = 3
ROWS = OWN * CHIPS
TAIL = 128 - ROWS
ROW_MAIN = 176
HID_MAIN = 288
CHUNKS = D // 128
PLANE_FEAT = NX * CHIP_FEAT
PLANE_CAP = NX * CHIP_CAP
X_ORDER = (0, 3, 1, 2)
TILE = 512
EXPERT = ("z", "x", "c")
Z_ORDER = (0, 7, 1, 6, 2, 5, 3, 4, 4)
BF = jnp.bfloat16
F32 = jnp.float32


def send(value, axis, size, by):
    return lax.ppermute(value, axis, [(i, (i + by) % size) for i in range(size)])


def together(*values):
    return lax.optimization_barrier(values)


def gather_chips(shard, ties=()):
    four = jnp.stack([shard] + [send(shard, "x", NX, by) for by in (1, 3, 2)])
    tied = []
    if ties:
        four, first = together(four, ties[0])
        tied.append(first)
    pieces, up, down = [four], four, four
    for step in range(3):
        up, down = send(up, "z", NZ, 1), send(down, "z", NZ, -1)
        if step + 1 < len(ties):
            up, down, one = together(up, down, ties[step + 1])
            tied.append(one)
        pieces += [up, down]
    return pieces + [send(up[:2], "z", NZ, 1), send(down[2:], "z", NZ, -1)], tied


def each_shard(place, pieces, body):
    for i, piece in enumerate(pieces):
        plane = lax.rem(place[0] + Z_ORDER[i], NZ) * NX
        for j in range(piece.shape[0]):
            x = lax.rem(place[1] + X_ORDER[j + (2 if i == 8 else 0)], NX)
            body(plane + x, piece[j])


def pack(full, main, extra=()):
    parts = [full[main:, k : k + TAIL] for k in range(0, ROWS, TAIL)]
    parts += [row[:, k : k + TAIL] for row in extra for k in range(0, ROWS, TAIL)]
    missing = main - sum(part.shape[0] for part in parts)
    if missing:
        parts.append(jnp.zeros((missing, TAIL), full.dtype))
    return jnp.concatenate([full[:main, :ROWS], jnp.concatenate(parts, axis=0)], axis=1)


def unpack(place, piece, first, plane, size, main, extra=None):
    rest = size - main
    for j in range(piece.shape[0]):
        shard = piece[j]
        at = pl.multiple_of(lax.rem(place[1] + X_ORDER[first + j], NX) * size, 16)
        plane[pl.ds(at, main), :] = shard[:main]
        parts = [shard[k * rest : (k + 1) * rest, ROWS:] for k in range(3)]
        plane[pl.ds(pl.multiple_of(at + main, 16), rest), :] = jnp.concatenate(
            parts + parts[:1], axis=1
        )
        if extra is not None:
            extra[...] += shard[3 * rest : 3 * rest + 16].astype(F32)


def plane_copies(place, planes, width, sources, held, sems):
    copies = []
    for i, plane in enumerate(planes):
        at = pl.multiple_of(lax.rem(place[0] + Z_ORDER[plane], NZ) * width, 128)
        copies.append([
            pltpu.make_async_copy(source.at[:, pl.ds(at, width)], held.at[i, k], sems.at[i, k])
            for k, source in enumerate(sources)
        ])
    for row in copies:
        for copy in row:
            copy.start()
    return copies


HALF = D // 2


def weight_copies(sources, held, sems):
    return [
        [
            pltpu.make_async_copy(
                source.at[:, pl.ds(half * HALF, HALF)],
                held.at[k, :, pl.ds(half * HALF, HALF)],
                sems.at[half, k],
            )
            for k, source in enumerate(sources)
        ]
        for half in range(2)
    ]


def experts(whole, square, copies, held, slot_weight, core, both):
    totals = [jnp.zeros((CAP, 128), F32) for _ in range(4)]
    for half in range(2):
        for copy in copies[half]:
            copy.wait()
        for at in range(half * HALF, (half + 1) * HALF, TILE):
            part = whole[at : at + TILE]
            for k in range(4):
                totals[k] += jnp.dot(held[k, :, at : at + TILE], part, preferred_element_type=F32)
    return activated(totals, square, slot_weight, core, both)


def activated(totals, square, slot_weight, core, both):
    scale = lax.rsqrt(square * (1.0 / D) + 1e-06)
    for k in range(2):
        first, second = totals[2 * k] * scale, totals[2 * k + 1] * scale
        at = pl.multiple_of((core if k == 0 else 1 - core) * CAP, 8)
        both[pl.ds(at, CAP), :] = first * (1.0 / (1.0 + jnp.exp(-first))) * second
    return both[...] * slot_weight


def first_kernel(place, *refs):
    pieces, weights = refs[:9], refs[9:13]
    slot_expert, gain, out, current, slot_weight, rows, turn, whole, both, held, sems = refs[13:]
    copies = weight_copies(weights, held, sems)
    for copy in copies[0] + copies[1]:
        copy.start()

    def body(chip, shard):
        rows[pl.ds(pl.multiple_of(chip * ROW_MAIN, 8), ROW_MAIN), :] = shard.astype(F32)

    each_shard(place, pieces, body)

    def chunk(at):
        parts = [rows[pl.ds(at + step, CHIPS, stride=ROW_MAIN), :] for step in (0, CHUNKS, 2 * CHUNKS)]
        parts.append(jnp.zeros((TAIL, 128), F32))
        return jnp.concatenate(parts, axis=0)

    square = jnp.zeros((128, 128), F32)
    for k in range(CHUNKS):
        values = chunk(k)
        square += values * values
        whole[k * 128 : (k + 1) * 128, :] = (values * gain[k : k + 1, :]).T.astype(BF)
    square = jnp.sum(square.T, axis=0, keepdims=True)
    picks = [rows[pl.ds(OWN * CHUNKS + t, CHIPS, stride=ROW_MAIN), :] for t in range(OWN)]
    weight = jnp.concatenate(picks + [jnp.zeros((TAIL, 128), F32)], axis=0).T
    expert = slot_expert[...]
    slots = jnp.zeros((CHIP_CAP, 128), F32)
    for k in range(FLIGHT):
        slots += jnp.where(expert == k, weight[k : k + 1], 0.0)
    slot_weight[...] = slots
    at = (place[0] * NX + place[1]) * CHIP_FEAT
    base = jnp.minimum(at // 128, CHUNKS - 3)
    for k in range(3):
        turn[k * 128 : (k + 1) * 128, :] = chunk(base + k).T
    current[...] = turn[pl.ds(pl.multiple_of(at - base * 128, 8), CHIP_FEAT), :].astype(BF)
    hidden = experts(whole, square, copies, held, slots, place[2], both)
    out[...] = pack(hidden, HID_MAIN).astype(BF)


def gate_up_kernel(place, *refs):
    pieces, weights = refs[:9], refs[9:13]
    slot_weight, out, extra, whole, both, held, sems = refs[13:]
    copies = weight_copies(weights, held, sems)
    for copy in copies[0] + copies[1]:
        copy.start()
    extra[...] = jnp.zeros(extra.shape, F32)
    for i, piece in enumerate(pieces):
        base = pl.multiple_of(lax.rem(place[0] + Z_ORDER[i], NZ) * PLANE_FEAT, 128)
        plane = whole.at[pl.ds(base, PLANE_FEAT)]
        unpack(place, piece, 2 if i == 8 else 0, plane, CHIP_FEAT, ROW_MAIN, extra)
    sums = extra[0:3, ROWS:] + extra[3:6, ROWS:]
    square = jnp.concatenate([sums[0:1], sums[1:2], sums[2:3], sums[0:1]], axis=1)
    hidden = experts(whole, square, copies, held, slot_weight[...], place[2], both)
    out[...] = pack(hidden, HID_MAIN).astype(BF)


def whole_update_kernel(place, *refs):
    pieces, picked = refs[:9], refs[9:11]
    current, gain, out, packed, whole, both, held, sems = refs[11:]
    copies = [pltpu.make_async_copy(picked[k], held.at[k], sems.at[k]) for k in range(2)]
    for copy in copies:
        copy.start()
    for i, piece in enumerate(pieces):
        base = pl.multiple_of(lax.rem(place[0] + Z_ORDER[i], NZ) * PLANE_CAP, 128)
        plane = whole.at[pl.ds(base, PLANE_CAP)]
        unpack(place, piece, 2 if i == 8 else 0, plane, CHIP_CAP, HID_MAIN)
    for k, copy in enumerate(copies):
        copy.wait()
        total = jnp.zeros((FEAT, 128), F32)
        for at in range(0, CHIPS * CHIP_CAP, TILE):
            total += jnp.dot(
                held[k, :, at : at + TILE], whole[at : at + TILE], preferred_element_type=F32
            )
        at = pl.multiple_of((place[2] if k == 0 else 1 - place[2]) * FEAT, 8)
        both[pl.ds(at, FEAT), :] = total
    fresh = (current[...].astype(F32) + both[...]).astype(BF)
    out[...] = fresh
    fresh = fresh.astype(F32)
    square = jnp.sum(fresh * fresh, axis=0, keepdims=True)
    high = square.astype(BF).astype(F32)
    packed[...] = pack(fresh * gain[...], ROW_MAIN, (high, square - high)).astype(BF)


def update_kernel(place, *refs):
    pieces, picked = refs[:7], refs[7:9]
    out, planes, held, sems = refs[9:]
    copies = plane_copies(place, range(7), PLANE_CAP, picked, held, sems)
    totals = [jnp.zeros((FEAT, 128), F32) for _ in range(2)]
    for i in range(7):
        unpack(place, pieces[i], 0, planes.at[i], CHIP_CAP, HID_MAIN)
        for k in range(2):
            copies[i][k].wait()
            totals[k] += jnp.dot(held[i, k], planes[i], preferred_element_type=F32)
    for k in range(2):
        out[k] = totals[k]


def update_last_kernel(place, *refs):
    pieces, picked = refs[:2], refs[2:4]
    before, current, gain, out, packed, both, plane, held, sems = refs[4:]
    copies = plane_copies(place, (7,), PLANE_CAP, picked, held, sems)
    for i in range(2):
        unpack(place, pieces[i], 2 * i, plane, CHIP_CAP, HID_MAIN)
    for k in range(2):
        copies[0][k].wait()
        total = before[k] + jnp.dot(held[0, k], plane[...], preferred_element_type=F32)
        at = pl.multiple_of((place[2] if k == 0 else 1 - place[2]) * FEAT, 8)
        both[pl.ds(at, FEAT), :] = total
    fresh = (current[...].astype(F32) + both[...]).astype(BF)
    out[...] = fresh
    fresh = fresh.astype(F32)
    square = jnp.sum(fresh * fresh, axis=0, keepdims=True)
    high = square.astype(BF).astype(F32)
    packed[...] = pack(fresh * gain[...], ROW_MAIN, (high, square - high)).astype(BF)


def pick_kernel(replica, slot_units, b0, b1, b2, b3, out, slab):
    for by, block in zip((0, 1, 3, 2), (b0, b1, b2, b3)):
        at = lax.rem(replica[0] + NY - by, NY) * BLOCK
        slab[:, pl.ds(pl.multiple_of(at, BLOCK), BLOCK)] = block[...]
    slab[:, UNITS:] = jnp.zeros((FEAT, 256), BF)
    lane = lax.broadcasted_iota(jnp.int32, (FEAT, 128), 1)

    def window(owner, lead):
        start = slot_units[owner * CAP]
        base = start // 128
        off = start - base * 128
        tiles = []
        for k in range(3):
            tile = slab[:, pl.ds(pl.multiple_of((base + k) * 128, 128), 128)].astype(F32)
            tiles.append(pltpu.roll(tile, lax.rem(128 - off + lead, 128), 1))
        return off, tiles

    def pair(p, carry):
        off, (r0, r1, r2) = window(2 * p, 0)
        out0 = jnp.where(lane < 128 - off, r0, r1)
        out1 = jnp.where(lane < 128 - off, r1, r2)
        off, (r0, r1, r2) = window(2 * p + 1, 64)
        late = jnp.where(lane < 192 - off, r0, r1)
        out2 = jnp.where(lane < 64 - off, r0, jnp.where(lane < 192 - off, r1, r2))
        out1 = jnp.where(lane < 64, out1, late)
        both = jnp.concatenate([out0, out1, out2], axis=1).astype(BF)
        out[:, pl.ds(pl.multiple_of(p * 384, 384), 384)] = both
        return carry

    lax.fori_loop(0, OWNERS // 2, pair, 0)


SMEM = pl.BlockSpec(memory_space=pltpu.SMEM)
VMEM = pl.BlockSpec(memory_space=pltpu.VMEM)
FAR = pl.BlockSpec(memory_space=pl.ANY)


def shape(*dims, dtype=BF):
    return jax.ShapeDtypeStruct(dims, dtype)


def call(kernel, outs, scratch, vmem, flops, moved_bytes, scalars, near, far=(), last=()):
    return pl.pallas_call(
        kernel,
        out_shape=outs,
        in_specs=[SMEM] * len(scalars) + [VMEM] * len(near) + [FAR] * len(far) + [VMEM] * len(last),
        out_specs=jax.tree.map(lambda _: VMEM, outs),
        scratch_shapes=scratch,
        compiler_params=pltpu.CompilerParams(vmem_limit_bytes=vmem * 1024 * 1024),
        cost_estimate=pl.CostEstimate(flops=flops, bytes_accessed=moved_bytes, transcendentals=0),
    )(*scalars, *near, *far, *last)


GATE_SCRATCH = [
    pltpu.VMEM((D, 128), BF),
    pltpu.VMEM((CHIP_CAP, 128), F32),
    pltpu.VMEM((4, CAP, D), BF),
    pltpu.SemaphoreType.DMA((2, 4)),
]


UPDATE_SCRATCH = [
    pltpu.VMEM((CHIPS * CHIP_CAP, 128), BF),
    pltpu.VMEM((CHIP_FEAT, 128), F32),
    pltpu.VMEM((2, FEAT, CHIPS * CHIP_CAP), BF),
    pltpu.SemaphoreType.DMA((2,)),
]


def plane_scratch(planes, width, sources, rows):
    lead = (planes,) if planes > 1 else ()
    return [
        pltpu.VMEM(lead + (width, 128), BF),
        pltpu.VMEM((planes, sources, rows, width), BF),
        pltpu.SemaphoreType.DMA((planes, sources)),
    ]


GATE_FLOPS = 2 * 2 * CHIP_CAP * D * 128
UPDATE_FLOPS = 2 * CHIP_FEAT * CHIPS * CHIP_CAP * 128


def local(
    learner_hidden,
    learner_cot,
    master,
    moment_one,
    moment_two,
    slot_units,
    gate_slots,
    up_slots,
    norm_gain,
    tokens,
    routes,
    gate_weights,
):
    replica = lax.axis_index("dp")
    z, x, c = (lax.axis_index(axis) for axis in EXPERT)
    place = jnp.stack([z, x, c]).astype(jnp.int32)
    chip = z * NX + x

    expert_ids = jnp.arange(FLIGHT, dtype=jnp.int32)
    picks = (routes[:, :, None] == expert_ids[None, None, :]).astype(F32)
    weight = jnp.sum(gate_weights.astype(F32)[:, :, None] * picks, axis=1).astype(BF)
    below = jnp.pad(weight, ((0, ROW_MAIN - OWN * CHUNKS - OWN), (0, 128 - FLIGHT)))
    packed = jnp.concatenate([tokens.reshape(OWN * CHUNKS, 128), below], axis=0)

    grad = lax.dot_general(
        learner_hidden, learner_cot, (((0,), (0,)), ((), ())), preferred_element_type=F32
    )
    grad = grad.astype(BF)

    def block_for(by):
        return lax.dynamic_slice_in_dim(grad, (replica + by) % NY * BLOCK, BLOCK, 0)

    outgoing = [block_for(by) for by in (1, 3, 2)]
    packed, *outgoing = together(packed, *outgoing)
    arriving = [send(block, "dp", NY, by) for block, by in zip(outgoing, (1, 3, 2))]
    pieces, arriving = gather_chips(packed, arriving)
    grad = sum(part.astype(F32) for part in [block_for(0), *arriving])
    moment_new = 0.9 * moment_one + 0.1 * grad
    second_new = 0.95 * moment_two + 0.05 * grad * grad
    corr_first = 1.0 - 0.9**ADAM_STEP
    corr_second = 1.0 - 0.95**ADAM_STEP
    master_new = master - 0.005 * (
        moment_new / corr_first / (jnp.sqrt(second_new / corr_second) + 1e-08) + 0.1 * master
    )
    slab = master_new.astype(BF).T

    weights = [gate_slots, up_slots] + [send(own, "c", NC, 1) for own in (gate_slots, up_slots)]
    gain = norm_gain.astype(F32)
    chip_gain = lax.dynamic_slice_in_dim(gain, chip * CHIP_FEAT, CHIP_FEAT)[:, None]
    chip_slots = lax.dynamic_slice_in_dim(slot_units, chip * CHIP_CAP, CHIP_CAP)
    slot_expert = jnp.where(chip_slots < UNITS, chip_slots // FF, -1)[:, None]
    hidden, current, slot_weight = call(
        first_kernel,
        (shape(HID_MAIN, 128), shape(CHIP_FEAT, 128), shape(CHIP_CAP, 128, dtype=F32)),
        [pltpu.VMEM((CHIPS * ROW_MAIN, 128), F32), pltpu.VMEM((384, 128), F32)] + GATE_SCRATCH,
        28,
        GATE_FLOPS,
        13_000_000,
        [place], pieces, weights, [slot_expert, gain.reshape(CHUNKS, 128)],
    )
    hidden, slab = together(hidden, slab)
    blocks = [send(slab, "dp", NY, by) for by in (1, 3, 2)]
    for step_index in range(STEPS):
        if step_index:
            pieces, _ = gather_chips(packed)
            hidden = call(
                gate_up_kernel,
                shape(HID_MAIN, 128),
                [pltpu.VMEM((16, 128), F32)] + GATE_SCRATCH,
                24,
                GATE_FLOPS,
                13_000_000,
                [place], pieces, weights, [slot_weight],
            )
        pieces, tied = gather_chips(hidden, () if step_index else blocks)
        if step_index == 0:
            own_picked = call(
                pick_kernel,
                shape(FEAT, OWNERS * CAP),
                [pltpu.VMEM((FEAT, UNITS + 256), BF)],
                14,
                0,
                5_000_000,
                [lax.axis_index("dp").astype(jnp.int32)[None], slot_units], [slab, *tied],
            )
            picked = [own_picked, send(own_picked, "c", NC, 1)]
            current, packed = call(
                whole_update_kernel,
                (shape(CHIP_FEAT, 128), shape(ROW_MAIN, 128)),
                UPDATE_SCRATCH,
                18,
                UPDATE_FLOPS,
                8_000_000,
                [place], pieces, picked, [current, chip_gain],
            )
            continue
        before = call(
            update_kernel,
            shape(2, FEAT, 128, dtype=F32),
            plane_scratch(7, PLANE_CAP, 2, FEAT),
            18,
            UPDATE_FLOPS * 7 // 8,
            7_000_000,
            [place], pieces[:7], picked,
        )
        current, packed = call(
            update_last_kernel,
            (shape(CHIP_FEAT, 128), shape(ROW_MAIN, 128)),
            [pltpu.VMEM((CHIP_FEAT, 128), F32)] + plane_scratch(1, PLANE_CAP, 2, FEAT),
            8,
            UPDATE_FLOPS // 8,
            1_500_000,
            [place], pieces[7:], picked, [before, current, chip_gain],
        )
    back = current[:, :ROWS].T.reshape(OWN, CHIPS, CHIP_FEAT).transpose(1, 0, 2)
    back = lax.all_to_all(back, ("z", "x"), split_axis=0, concat_axis=0, tiled=True)
    decoded = back.transpose(1, 0, 2).reshape(OWN, D)
    return (master_new, moment_new, second_new, decoded)


def solution(mesh):
    mesh = jax.sharding.Mesh(mesh.devices.reshape(NY, NZ, NX, NC), ("dp",) + EXPERT)
    placed = (
        P("dp", None),
        P("dp", EXPERT),
        P("dp", EXPERT),
        P("dp", EXPERT),
        P("dp", EXPERT),
        P(),
        P(EXPERT, None),
        P(EXPERT, None),
        P(),
        P(("dp",) + EXPERT, None),
        P(("dp",) + EXPERT, None),
        P(("dp",) + EXPERT, None),
    )
    return jax.shard_map(
        local,
        mesh=mesh,
        in_specs=placed,
        out_specs=(
            P("dp", EXPERT),
            P("dp", EXPERT),
            P("dp", EXPERT),
            P(("dp",) + EXPERT, None),
        ),
        check_vma=False,
    )
```
